256 devices in a mesh: slab: 64 (over z, x, y_lo), col: 4 (over y_hi, core).
Axes of the slice: x: 4, y: 4 (y_hi: 2, y_lo: 2; y = y_hi * 2 + y_lo), z: 8, core: 2. Of those that a mesh axis runs over, the one named last changes fastest.
Arguments:
- displacement: float32 [6, 512, 64, 256], P(None, 'slab', 'col'), may hold values from -1.2 to 1.2
- species: int32 [512, 64, 256], P('slab', 'col'), may hold values from 0 to 1, as said below
- step_sizes: float32 [3], replicated, may hold values from 0.1 to 0.3
Outputs:
- relaxed: float32 [6, 512, 64, 256], P(None, 'slab', 'col')
- energies: float32 [3], replicated
The draws below stay inside these ranges and needn't reach their ends.
Inputs may be any that keep to these rules, and one draw needn't show every extreme that they name: `species`: 0 marks an indium cation, 1 a gallium cation; every anion is arsenic.
All inputs are finite; a program needn't handle non-finite values.
Results may differ from the reference program's by a relative error of at most 0.0055.
Values sent between devices are 32-bit elements; how exact they have to be, the bound alone decides.
No kernel may reach another device: no remote copies, remote signals or barrier semaphores. Data moves between devices by JAX's collectives and lax.ppermute only.
A program may use at most 64 MiB of HBM per device.

```python
import math
import jax
import jax.numpy as jnp

CZ = 8
CY = 16
NX = 256
ITERS = 3
NZ = 512
NY = 64


def block_cells(values):
    return jnp.repeat(jnp.repeat(values, CZ, axis=-2), CY, axis=-1)[..., None]


def draw_species(key, part):
    key = jax.random.fold_in(key, 23)
    first, second = jax.random.split(key)
    share = jax.random.randint(first, (NZ // CZ, NY // CY), 1, 16)
    share_cells = block_cells(share)
    votes = jax.random.randint(second, (NZ, NY, NX), 0, 16)
    return jnp.where(votes < share_cells, 0, 1).astype(jnp.int32)


def wave_field(random_keys, level_lo, level_hi):
    block_groups = (NZ // CZ, NY // CY)
    ripple_level = jnp.exp(jax.random.uniform(random_keys[0], block_groups, jnp.float32, level_lo, level_hi))
    wave_x = block_cells(jax.random.randint(random_keys[1], block_groups, 1, 8))
    wave_y = block_cells(jax.random.randint(random_keys[2], block_groups, 1, 8))
    wave_z = block_cells(jax.random.randint(random_keys[3], block_groups, 1, 8))
    phases = block_cells(jax.random.uniform(random_keys[4], (6,) + block_groups, jnp.float32, -math.pi, math.pi))
    z_index = jnp.arange(NZ, dtype=jnp.int32)[:, None, None]
    y_index = jnp.arange(NY, dtype=jnp.int32)[None, :, None]
    x_index = jnp.arange(NX, dtype=jnp.int32)[None, None, :]
    turns = (wave_x * x_index + wave_y * y_index + wave_z * z_index) % 16
    angle = 2.0 * math.pi / 16.0 * turns.astype(jnp.float32)
    wave = 1.4142135 * jnp.sin(angle[None] + phases)
    return block_cells(ripple_level)[None] * wave


def draw_displacement(key, part):
    key = jax.random.fold_in(key, 11)
    random_keys = jax.random.split(key, 10)
    block_groups = (NZ // CZ, NY // CY)
    shape = (6, NZ, NY, NX)
    rough = jax.random.normal(random_keys[0], shape, jnp.float32)
    coarse_level = jnp.exp(jax.random.uniform(random_keys[1], block_groups, jnp.float32, -1.5, 1.3))
    waves = wave_field(random_keys[3:8], -1.5, 1.3)
    field = 0.09 * (block_cells(coarse_level)[None] * rough + waves)
    return jnp.clip(field, -1.2, 1.2).astype(jnp.float32)


def setup_inputs(seed: int = 0) -> dict:
    key_list = jax.random.split(jax.random.key(seed), 4)
    return {
        "displacement": draw_displacement(jax.random.fold_in(key_list[3], 71), 0),
        "species": draw_species(jax.random.fold_in(key_list[3], 71), 0),
        "step_sizes": jnp.clip(jnp.exp(jax.random.uniform(key_list[2], (ITERS,), jnp.float32, math.log(0.1), math.log(0.3))), 0.1, 0.3),
    }


bond_unit = 4.0 / 3.0 ** 0.5
bond_signs = ((1.0, 1.0, 1.0), (1.0, -1.0, -1.0), (-1.0, 1.0, -1.0), (-1.0, -1.0, 1.0))
neighbour_offsets = ((0, 0, 0), (0, 0, 1), (0, 1, 0), (1, 0, 0))

def constants(species):
    indium = species == 0
    alpha_cell = jnp.where(indium, 0.848, 1.0).astype(jnp.float32)
    beta_cell = jnp.where(indium, 0.132, 0.215).astype(jnp.float32)
    length_total = jnp.where(indium, 4.28, 4.0).astype(jnp.float32)
    return jnp.stack([alpha_cell, beta_cell, length_total])

def behind_cell(field, offset):
    return jnp.roll(field, offset, axis=(0, 1, 2))

def ahead_cell(field, offset):
    return jnp.roll(field, (-offset[0], -offset[1], -offset[2]), axis=(0, 1, 2))

def cell_energy(field_ext, constants_ext, behind, ahead):
    anchor = (0, 0, 0)
    own_cation = [ahead(field_ext[m], anchor) for m in range(3)]
    own_anion = [ahead(field_ext[3 + m], anchor) for m in range(3)]
    alpha_cell = ahead(constants_ext[0], anchor)
    beta_cell = ahead(constants_ext[1], anchor)
    length_total = ahead(constants_ext[2], anchor)
    square = length_total * length_total
    bonds = []
    for j in range(4):
        offset = neighbour_offsets[j]
        bonds.append([bond_unit * bond_signs[j][m] + behind(field_ext[3 + m], offset) - own_cation[m] for m in range(3)])
    energy = jnp.zeros_like(square)
    for j in range(4):
        length_sq = bonds[j][0] ** 2 + bonds[j][1] ** 2 + bonds[j][2] ** 2
        energy = energy + 0.1875 * alpha_cell / square * (length_sq - square) ** 2
    for j in range(4):
        for l in range(j + 1, 4):
            inner_sum = bonds[j][0] * bonds[l][0] + bonds[j][1] * bonds[l][1] + bonds[j][2] * bonds[l][2]
            energy = energy + 0.375 * beta_cell / square * (inner_sum + square / 3.0) ** 2
    anion_arms = []
    arm_lengths = []
    arm_betas = []
    for j in range(4):
        offset = neighbour_offsets[j]
        anion_arms.append([-bond_unit * bond_signs[j][m] + ahead(field_ext[m], offset) - own_anion[m] for m in range(3)])
        arm_betas.append(ahead(constants_ext[1], offset))
        arm_lengths.append(ahead(constants_ext[2], offset))
    for j in range(4):
        for l in range(j + 1, 4):
            inner_sum = anion_arms[j][0] * anion_arms[l][0] + anion_arms[j][1] * anion_arms[l][1] + anion_arms[j][2] * anion_arms[l][2]
            length_prod = arm_lengths[j] * arm_lengths[l]
            energy = energy + 0.1875 * (arm_betas[j] + arm_betas[l]) / length_prod * (inner_sum + length_prod / 3.0) ** 2
    return energy

def reference(displacement, species, step_sizes):
    constants_all = constants(species)
    cell_count = displacement.shape[1] * displacement.shape[2] * displacement.shape[3]

    def total_energy(field):
        return jnp.sum(cell_energy(field, constants_all, behind_cell, ahead_cell))
    position = displacement
    energies = []
    direction = None
    gradient_prev = None
    norm_prev = None
    for iteration in range(ITERS):
        energy, gradient = jax.value_and_grad(total_energy)(position)
        norm_now = jnp.sum(gradient * gradient)
        if iteration == 0:
            direction = -gradient
        else:
            beta_ratio = (norm_now - jnp.sum(gradient * gradient_prev)) / (norm_prev + 1e-06)
            direction = beta_ratio * direction - gradient
        position = position + step_sizes[iteration] * direction
        gradient_prev = gradient
        norm_prev = norm_now
        energies.append(energy / cell_count)
    return (position, jnp.stack(energies))
```

```python
import functools

import jax
import jax.numpy as jnp
from jax import lax
from jax.experimental import pallas as pl
from jax.experimental.pallas import tpu as pltpu
from jax.sharding import PartitionSpec as P

CZ, CY, NX = 8, 16, 256
W = 3
ZE = CZ + 2 * W
IE = 4 + 2 * W
ROWS = (-3, -2, -1, 16, 17, 18)
PLANE = 7 * CY + 6 * 8
H = 4.0 / 3.0**0.5
SIGNS = ((1, 1, 1), (1, -1, -1), (-1, 1, -1), (-1, -1, 1))
PAIRS = ((0, 1), (0, 2), (0, 3), (1, 2), (1, 3), (2, 3))
SAMPLES = (-1.0, 0.0, 1.0, 2.0)
E0, E1, ES, N0, N1, X1, GG1, GG0, GG = 0, 1, 2, 6, 7, 8, 9, 13, 17
GPAIRS = tuple((k, l) for k in range(4) for l in range(k, 4))
SUMS = 32
MIB = 1024 * 1024
f32 = jnp.float32


def halves():
    return (0, slice(0, 128)), (1, slice(128, NX))


def pack_y(disp, spec, up, down, rows0, rows1):
    for h, at in halves():
        rows = (rows0, rows1)[h]
        rows[0 : 6 * CZ * CY, :] = disp[:, at]
        rows[6 * CZ * CY : 7 * CZ * CY, :] = spec[:, at].astype(f32)
        rows[7 * CZ * CY :, :] = jnp.zeros((CZ * CY, 128), f32)
        for dst, first in ((up, CY - W), (down, 0)):
            for r in range(W):
                for z in range(CZ):
                    to = (r * CZ + z) * 8
                    dst[to : to + 8, at] = rows[pl.ds(z * CY + first + r, 8, stride=CZ * CY), :]


def y_halo(ylo, yhi, r, z, at=slice(None)):
    src = ylo if r < W else yhi
    return src[pl.ds((r % W) * CZ * 8 + z * 8, 8), at]


def pack_z(disp, spec, ylo, yhi, up, down):
    for dst, first in ((up, CZ - W), (down, 0)):
        for k in range(W):
            z = first + k
            base = k * PLANE
            for ch in range(6):
                at = (ch * CZ + z) * CY
                dst[base + ch * CY : base + (ch + 1) * CY, :] = disp[at : at + CY, :]
            dst[base + 6 * CY : base + 7 * CY, :] = spec[z * CY : (z + 1) * CY, :].astype(f32)
            for r in range(6):
                at = base + 7 * CY + r * 8
                dst[at : at + 8, :] = y_halo(ylo, yhi, r, z)


def lanes():
    return lax.broadcasted_iota(jnp.int32, (8, 128), 1)


def x_before(v):
    r = pltpu.roll(v, 1, 1)
    return jnp.where(lanes() == 0, pltpu.roll(r, 4, 0), r)


def x_after(v):
    r = pltpu.roll(v, 127, 1)
    return jnp.where(lanes() == 127, pltpu.roll(r, 4, 0), r)


def dot(a, b):
    return a[0] * b[0] + a[1] * b[1] + a[2] * b[2]


def loop(lo, hi, body):
    def step(z, carry):
        body(z)
        return carry

    lax.fori_loop(lo, hi, step, 0)


def fill_plane(field, both, z, natural, halo):
    for h, at in halves():
        rows = both[h]
        for ch in range(7):
            rows[ch * 32 + 8 : ch * 32 + 24, :] = natural(ch, at)
        for r, y in enumerate(ROWS):
            rows[pl.ds(y + 8, 8, stride=32), :] = halo(r, at)
        for ch in range(7):
            for i in range(IE):
                first = ch * 32 + 8 - W + i
                field[ch, z, i, 4 * h : 4 * h + 4, :] = rows[pl.ds(first, 4, stride=4), :]


def constants(field, kc, ka, kl):
    def cation(z):
        for i in range(1, IE):
            indium = field[6, z, i] < 0.5

            def pick(fn):
                return jnp.where(indium, fn(0.848, 0.132, 4.28), fn(1.0, 0.215, 4.0)).astype(f32)

            kc[0, z, i] = pick(lambda a, b, l: 0.75 * a / l**2)
            kc[1, z, i] = pick(lambda a, b, l: -0.75 * a)
            kc[2, z, i] = pick(lambda a, b, l: 0.75 * b / l**2)
            kc[3, z, i] = pick(lambda a, b, l: 0.25 * b)
            kc[4, z, i] = pick(lambda a, b, l: l**2 / (3.0 * a))
            kc[5, z, i] = pick(lambda a, b, l: l**2 / (1.5 * b))

    loop(1, ZE, cation)

    def anion(z):
        for i in range(0, IE - 1):
            s = (field[6, z, i], x_after(field[6, z, i]), field[6, z, i + 1], field[6, z + 1, i])
            for q, (j, l) in enumerate(PAIRS):
                t = s[j] + s[l]

                def pick(fn):
                    ii = fn(0.264, 4.28 * 4.28)
                    mixed = fn(0.347, 4.28 * 4.0)
                    gg = fn(0.43, 16.0)
                    return jnp.where(t < 0.5, ii, jnp.where(t < 1.5, mixed, gg)).astype(f32)

                ka[q, z, i] = pick(lambda b, ll: 0.375 * b / ll)
                ka[6 + q, z, i] = pick(lambda b, ll: 0.125 * b)
                kl[q, z, i] = pick(lambda b, ll: ll / 3.0)

    loop(0, ZE - 1, anion)


def gradient(field, out, zs, cells, e_row, refs, zo, io):
    bs, fs, rs, kc, ka, kl, acc = refs
    (za, zb), (ia, ib) = zs, cells
    offsets = ((0, 0), (0, 0), (0, 1), (1, 0))

    def bonds(z, i, which):
        found = {}
        cat = [field[m, z, i] for m in range(3)]
        lo, hi = [c - H for c in cat], [c + H for c in cat]
        for j in which:
            dz, di = offsets[j]
            b = []
            for m in range(3):
                a = field[3 + m, z - dz, i - di]
                if j == 1:
                    a = x_before(a)
                b.append(a - (lo[m] if SIGNS[j][m] > 0 else hi[m]))
            found[j] = b
        return found

    def keep(z, i, b, which):
        for j in which:
            for m in range(3):
                bs[3 * j + m, z, i] = b[j][m]

    def cation(z, i, which, energy):
        b = bonds(z, i, range(4))
        kd, md, kb, mb = (kc[n, z, i] for n in range(4))
        e = {}
        for j in range(4):
            for l in range(j, 4):
                if j not in which and l not in which:
                    continue
                d = dot(b[j], b[l])
                e[j, l] = e[l, j] = kd * d + md if j == l else kb * d + mb
        f = {j: [sum(e[j, l] * b[l][m] for l in range(4)) for m in range(3)] for j in which}
        total = None
        if energy:
            diag = sum(e[j, j] * e[j, j] for j in range(4))
            off = sum(e[p] * e[p] for p in PAIRS)
            total = diag * kc[4, z, i] + off * kc[5, z, i]
        return b, f, total

    def anion(z, i, which, energy):
        b0 = [bs[m, z, i] for m in range(3)]
        b1 = [x_after(bs[3 + m, z, i]) for m in range(3)]
        b2 = [bs[6 + m, z, i + 1] for m in range(3)]
        b3 = [bs[9 + m, z + 1, i] for m in range(3)]
        b = (b0, b1, b2, b3)
        c, total = {}, None
        for q, (j, l) in enumerate(PAIRS):
            if j not in which and l not in which:
                continue
            d = dot(b[j], b[l])
            c[j, l] = c[l, j] = ka[q, z, i] * d + ka[6 + q, z, i]
            if energy:
                part = c[j, l] * (d + kl[q, z, i])
                total = part if total is None else total + part
        r = {j: [sum(c[j, l] * b[l][m] for l in range(4) if l != j) for m in range(3)] for j in which}
        return r, total

    def own(i):
        return W <= i < W + 4

    def bond_plane(z):
        b = bonds(z, ia - 1, (0, 1, 3))
        keep(z, ia - 1, b, (0, 1, 3))
        total = None
        for i in range(ia, ib + 1):
            b, f, e = cation(z, i, range(4), own(i))
            keep(z, i, b, range(4))
            for m in range(3):
                fs[m, z, i] = f[0][m] + f[1][m] + f[2][m] + f[3][m]
                fs[3 + m, z, i] = f[0][m] + x_after(f[1][m])
                fs[6 + m, z, i] = f[2][m]
                fs[9 + m, z, i] = f[3][m]
            if e is not None:
                total = e if total is None else total + e
        b, f, _ = cation(z, ib + 1, (2,), False)
        keep(z, ib + 1, b, (2,))
        for m in range(3):
            fs[6 + m, z, ib + 1] = f[2][m]
        inside = jnp.logical_and(z >= W, z < W + CZ)
        acc[e_row] += jnp.where(inside, total, 0.0)

    loop(za, zb + 1, bond_plane)

    b = bonds(zb + 1, ia - 1, (3,))
    keep(zb + 1, ia - 1, b, (3,))
    for i in range(ia, ib + 1):
        b, f, _ = cation(zb + 1, i, (3,), False)
        keep(zb + 1, i, b, (3,))
        for m in range(3):
            fs[9 + m, zb + 1, i] = f[3][m]

    for i in range(ia, ib + 2):
        which = ((0, 1) if i <= ib else ()) + ((2,) if i > ia else ())
        keep(za - 1, i, bonds(za - 1, i, which), which)
    for i in range(ia, ib + 1):
        r, _ = anion(za - 1, i, (3,), False)
        for m in range(3):
            rs[m, za - 1, i] = r[3][m]

    def anion_plane(z):
        r, _ = anion(z, ia - 1, (2,), False)
        before = r[2]
        total = None
        for i in range(ia, ib + 1):
            r, e = anion(z, i, range(4), own(i))
            for m in range(3):
                rs[m, z, i] = r[3][m]
                back = r[0][m] + x_before(r[1][m]) + before[m] + rs[m, z - 1, i]
                out[m, z - zo, i - io] = -(fs[m, z, i] + back)
                ahead = fs[3 + m, z, i] + fs[6 + m, z, i + 1] + fs[9 + m, z + 1, i]
                out[3 + m, z - zo, i - io] = ahead + (r[0][m] + r[1][m] + r[2][m] + r[3][m])
            before = r[2]
            if e is not None:
                total = e if total is None else total + e
        inside = jnp.logical_and(z >= W, z < W + CZ)
        acc[e_row] += jnp.where(inside, 0.5 * total, 0.0)

    loop(za, zb + 1, anion_plane)


def relax(disp, spec, ylo, yhi, zlo, zhi, steps, fields, sums, field, rows0, rows1, g0, g1, bs, fs, rs, kc, ka, kl, acc):
    acc[...] = jnp.zeros_like(acc)

    def outer(src, z0):
        def plane(k):
            base = k * PLANE
            fill_plane(
                field,
                (rows0, rows1),
                z0 + k,
                lambda ch, at: src[pl.ds(base + ch * CY, CY), at],
                lambda r, at: src[pl.ds(base + 7 * CY + r * 8, 8), at],
            )

        loop(0, W, plane)

    outer(zlo, 0)
    outer(zhi, W + CZ)

    def inner(z):
        def natural(ch, at):
            if ch < 6:
                return disp[pl.ds(ch * CZ * CY + z * CY, CY), at]
            return spec[pl.ds(z * CY, CY), at].astype(f32)

        fill_plane(field, (rows0, rows1), W + z, natural, lambda r, at: y_halo(ylo, yhi, r, z, at))

    loop(0, CZ, inner)
    constants(field, kc, ka, kl)
    refs = (bs, fs, rs, kc, ka, kl, acc)

    gradient(field, g0, (1, ZE - 2), (1, IE - 2), E0, refs, 0, 0)
    s0, s1 = steps[0], steps[1]

    def first(z):
        for i in range(1, IE - 1):
            for ch in range(6):
                field[ch, z, i] = field[ch, z, i] - s0 * g0[ch, z, i]

    loop(1, ZE - 1, first)
    gradient(field, g1, (2, ZE - 3), (2, IE - 3), E1, refs, 0, 0)

    def second(z):
        for i in range(2, IE - 2):
            for ch in range(6):
                p, a = field[ch, z, i], g0[ch, z, i]
                if W <= i < W + 4:
                    fields[4, ch, jnp.clip(z - W, 0, CZ - 1), i - W] = p
                field[ch, z, i] = p - s1 * (g1[ch, z, i] - a)

    loop(2, W, second)
    loop(ZE - W, ZE - 2, second)
    loop(W, W + CZ, second)

    def sample(k, carry):
        gradient(field, fields.at[k], (W, W + CZ - 1), (W, W + 3), ES + k, refs, W, W)

        def onward(z):
            for i in range(2, IE - 2):
                for ch in range(6):
                    field[ch, z, i] = field[ch, z, i] - s1 * g0[ch, z, i]

        loop(2, ZE - 2, onward)
        return carry

    lax.fori_loop(0, 4, sample, 0)

    def products(z):
        part = [None] * SUMS

        def add(n, v):
            part[n] = v if part[n] is None else part[n] + v

        for i in range(4):
            for ch in range(6):
                a, b = g0[ch, z + W, i + W], g1[ch, z + W, i + W]
                g = [fields[k, ch, z, i] for k in range(4)]
                fields[5, ch, z, i] = a
                fields[6, ch, z, i] = b
                add(N0, a * a)
                add(N1, b * b)
                add(X1, a * b)
                for k in range(4):
                    add(GG1 + k, g[k] * b)
                    add(GG0 + k, g[k] * a)
                for n, (k, l) in enumerate(GPAIRS):
                    add(GG + n, g[k] * g[l])
        for n, v in enumerate(part):
            if v is not None:
                acc[n] += v

    loop(0, CZ, products)
    partial = jnp.sum(acc[...], axis=1)
    row = lax.broadcasted_iota(jnp.int32, (SUMS, 128), 0)
    lane = lax.broadcasted_iota(jnp.int32, (SUMS, 128), 1)
    spread = jnp.where(row == lane, jnp.sum(partial, axis=1, keepdims=True), 0.0)
    sums[...] = jnp.broadcast_to(jnp.sum(spread, axis=0, keepdims=True), sums.shape)


def finish(cell_count, gathered, steps, fields, out, energies, rows0, rows1):
    total = jnp.sum(gathered[...], axis=0, keepdims=True)

    def pick(n):
        return total[:, n : n + 1]

    t = (pick(N1) - pick(X1)) / (pick(N0) + 1e-06)
    lag = (
        -t * (t - 1.0) * (t - 2.0) * (1.0 / 6.0),
        (t + 1.0) * (t - 1.0) * (t - 2.0) * 0.5,
        -(t + 1.0) * t * (t - 2.0) * 0.5,
        (t + 1.0) * t * (t - 1.0) * (1.0 / 6.0),
    )
    t2, t3, t4 = t * t, t * t * t, t * t * t * t
    area = (
        -(t4 * 0.25 - t3 + t2) * (1.0 / 6.0),
        (t4 * 0.25 - t3 * (2.0 / 3.0) - t2 * 0.5 + 2.0 * t) * 0.5,
        -(t4 * 0.25 - t3 * (1.0 / 3.0) - t2) * 0.5,
        (t4 * 0.25 - t2 * 0.5) * (1.0 / 6.0),
    )
    norm2 = sum((1.0 if k == l else 2.0) * lag[k] * lag[l] * pick(GG + n) for n, (k, l) in enumerate(GPAIRS))
    cross2 = sum(lag[k] * pick(GG1 + k) for k in range(4))
    ratio = (norm2 - cross2) / (pick(N1) + 1e-06)
    s1, s2 = steps[1], steps[2]
    energy2 = pick(ES + 1) - s1 * sum(area[k] * pick(GG0 + k) for k in range(4))
    scale = 1.0 / cell_count
    energies[0] = jnp.sum(pick(E0)) * scale
    energies[1] = jnp.sum(pick(E1)) * scale
    energies[2] = jnp.sum(energy2) * scale
    along = s1 + s2 * ratio
    weights = [jnp.broadcast_to(w, (8, 128)) for w in [s2 * q for q in lag] + [along * t, along]]

    def plane(z):
        for ch in range(6):
            for i in range(4):
                v = fields[4, ch, z, i]
                for n, k in enumerate((0, 1, 2, 3, 5, 6)):
                    v = v - weights[n] * fields[k, ch, z, i]
                rows0[pl.ds(ch * CY + i, 4, stride=4), :] = v[0:4]
                rows1[pl.ds(ch * CY + i, 4, stride=4), :] = v[4:8]
        for ch in range(6):
            for h, at in halves():
                rows = (rows0, rows1)[h]
                out[pl.ds(ch * CZ * CY + z * CY, CY), at] = rows[ch * CY : (ch + 1) * CY, :]

    loop(0, CZ, plane)


def vmem():
    return pl.BlockSpec(memory_space=pltpu.VMEM)


def smem():
    return pl.BlockSpec(memory_space=pltpu.SMEM)


def params(mib):
    return pltpu.CompilerParams(vmem_limit_bytes=mib * MIB)


def ring(value, axis, step):
    n = lax.axis_size(axis)
    return lax.ppermute(value, axis, [(i, (i + step) % n) for i in range(n)])


def per_device(displacement, species, step_sizes):
    shape = jax.ShapeDtypeStruct
    devices = lax.axis_size("slab") * lax.axis_size("col")
    cell_count = devices * CZ * CY * NX
    disp = displacement.reshape(6 * CZ * CY, NX)
    spec = species.reshape(CZ * CY, NX)
    edge = shape((W * CZ * 8, NX), f32)
    up, down = pl.pallas_call(
        pack_y, out_shape=(edge, edge), in_specs=[vmem()] * 2, out_specs=[vmem()] * 2,
        scratch_shapes=[pltpu.VMEM((8 * CZ * CY, 128), f32)] * 2,
        name="pack_y",
    )(disp, spec)
    ylo, yhi = ring(up, "col", 1), ring(down, "col", -1)
    block = shape((W * PLANE, NX), f32)
    up, down = pl.pallas_call(
        pack_z, out_shape=(block, block), in_specs=[vmem()] * 4, out_specs=[vmem()] * 2, name="pack_z"
    )(disp, spec, ylo, yhi)
    zlo, zhi = ring(up, "slab", 1), ring(down, "slab", -1)

    def tiles(*lead):
        return pltpu.VMEM((*lead, 8, 128), f32)

    fields, sums = pl.pallas_call(
        relax,
        out_shape=(shape((7, 6, CZ, 4, 8, 128), f32), shape((devices, 128), f32)),
        in_specs=[vmem()] * 6 + [smem()],
        out_specs=[vmem()] * 2,
        scratch_shapes=[
            tiles(7, ZE, IE),
            pltpu.VMEM((8 * 32, 128), f32),
            pltpu.VMEM((8 * 32, 128), f32),
            tiles(6, ZE, IE),
            tiles(6, ZE, IE),
            tiles(12, ZE, IE),
            tiles(12, ZE, IE),
            tiles(3, ZE, IE),
            tiles(6, ZE, IE),
            tiles(12, ZE, IE),
            tiles(6, ZE, IE),
            tiles(SUMS),
        ],
        compiler_params=params(58),
        name="relax",
    )(disp, spec, ylo, yhi, zlo, zhi, step_sizes)
    gathered = lax.all_to_all(sums.reshape(devices, 1, 128), ("slab", "col"), 0, 0)
    relaxed, energies = pl.pallas_call(
        functools.partial(finish, cell_count),
        out_shape=(shape((6 * CZ * CY, NX), f32), shape((3,), f32)),
        in_specs=[vmem(), smem(), vmem()],
        out_specs=[vmem(), smem()],
        scratch_shapes=[pltpu.VMEM((6 * CY, 128), f32)] * 2,
        compiler_params=params(32),
        name="finish",
    )(gathered.reshape(devices, 128), step_sizes, fields)
    return relaxed.reshape(displacement.shape), energies


def solution(mesh):
    in_specs = (P(None, "slab", "col", None), P("slab", "col", None), P())
    out_specs = (P(None, "slab", "col", None), P())
    return jax.shard_map(
        per_device, mesh=mesh, in_specs=in_specs, out_specs=out_specs, check_vma=False
    )
```

```python
import functools

import jax
import jax.numpy as jnp
from jax import lax
from jax.experimental import pallas as pl
from jax.experimental.pallas import tpu as pltpu
from jax.sharding import PartitionSpec as P

CZ, CY, NX = 8, 16, 256
W = 3
ZE = CZ + 2 * W
IE = 4 + 2 * W
ROWS = (-3, -2, -1, 16, 17, 18)
PLANE = 7 * CY + 6 * 8
H = 4.0 / 3.0**0.5
SIGNS = ((1, 1, 1), (1, -1, -1), (-1, 1, -1), (-1, -1, 1))
PAIRS = ((0, 1), (0, 2), (0, 3), (1, 2), (1, 3), (2, 3))
SAMPLES = (-1.0, 0.0, 1.0, 2.0)
E0, E1, ES, N0, N1, X1, GG1, GG0, GG = 0, 1, 2, 6, 7, 8, 9, 13, 17
GPAIRS = tuple((k, l) for k in range(4) for l in range(k, 4))
SUMS = 32
BLOCKS = ((6, 7), (0, 1), (5,), (2,))
MIB = 1024 * 1024
STATE = 10
f32 = jnp.float32


def halves():
    return (0, slice(0, 128)), (1, slice(128, NX))


def pack(disp, spec, yup, ydown, *outs):
    blocks, own = outs[:-2], outs[-2:]
    for h, at in halves():
        rows = own[h]
        rows[0 : 6 * CZ * CY, :] = disp[:, at]
        rows[6 * CZ * CY : 7 * CZ * CY, :] = spec[:, at].astype(f32)
        rows[7 * CZ * CY :, :] = jnp.zeros((CZ * CY, 128), f32)
        for dst, first in ((yup, CY - W), (ydown, 0)):
            for r in range(W):
                for z in range(CZ):
                    to = (r * CZ + z) * 8
                    dst[to : to + 8, at] = rows[pl.ds(z * CY + first + r, 8, stride=CZ * CY), :]
    for dst, planes in zip(blocks, BLOCKS):
        for k, z in enumerate(planes):
            for ch in range(7):
                to = k * PLANE + ch * CY
                for h, at in halves():
                    first = (ch * CZ + z) * CY
                    dst[to : to + CY, at] = own[h][first : first + CY, :]


def y_halo(ylo, yhi, r, z, at=slice(None)):
    src = ylo if r < W else yhi
    return src[pl.ds((r % W) * CZ * 8 + z * 8, 8), at]


def pack_halo(ylo, yhi, *refs):
    for dst, planes in zip(refs[len(BLOCKS) :], BLOCKS):
        for k, z in enumerate(planes):
            for r in range(6):
                to = k * PLANE + 7 * CY + r * 8
                dst[to : to + 8, :] = y_halo(ylo, yhi, r, z)


def lanes():
    return lax.broadcasted_iota(jnp.int32, (8, 128), 1)


def x_before(v):
    r = pltpu.roll(v, 1, 1)
    return jnp.where(lanes() == 0, pltpu.roll(r, 4, 0), r)


def x_after(v):
    r = pltpu.roll(v, 127, 1)
    return jnp.where(lanes() == 127, pltpu.roll(r, 4, 0), r)


def dot(a, b):
    return a[0] * b[0] + a[1] * b[1] + a[2] * b[2]


def loop(n, body, unroll=1):
    def step(k, carry):
        for q in range(unroll):
            body(k * unroll + q)
        return carry

    full = n // unroll
    if full > 1:
        lax.fori_loop(0, full, step, 0)
    else:
        full = 0
    for q in range(full * unroll, n):
        body(q)


def fill_plane(field, both, z, natural, halo):
    for h, at in halves():
        rows = both[h]
        for ch in range(7):
            rows[ch * 32 + 8 : ch * 32 + 24, :] = natural(ch, h, at)
        for r, y in enumerate(ROWS):
            rows[pl.ds(y + 8, 8, stride=32), :] = halo(r, at)
        for ch in range(7):
            for i in range(IE):
                first = ch * 32 + 8 - W + i
                field[ch, z, i, 4 * h : 4 * h + 4, :] = rows[pl.ds(first, 4, stride=4), :]


def fill_block(field, both, src, k, z):
    base = k * PLANE
    fill_plane(
        field,
        both,
        z,
        lambda ch, h, at: src[pl.ds(base + ch * CY, CY), at],
        lambda r, at: src[pl.ds(base + 7 * CY + r * 8, 8), at],
    )


def cation_constants(field, kc, z):
    for i in range(1, IE):
        indium = field[6, z, i] < 0.5

        def pick(fn):
            return jnp.where(indium, fn(0.848, 0.132, 4.28), fn(1.0, 0.215, 4.0)).astype(f32)

        kc[0, z, i] = pick(lambda a, b, l: 0.75 * a / l**2)
        kc[1, z, i] = pick(lambda a, b, l: -0.75 * a)
        kc[2, z, i] = pick(lambda a, b, l: 0.75 * b / l**2)
        kc[3, z, i] = pick(lambda a, b, l: 0.25 * b)
        kc[4, z, i] = pick(lambda a, b, l: l**2 / (3.0 * a))
        kc[5, z, i] = pick(lambda a, b, l: l**2 / (1.5 * b))


def anion_constants(field, ka, kl, z):
    for i in range(0, IE - 1):
        s = (field[6, z, i], x_after(field[6, z, i]), field[6, z, i + 1], field[6, z + 1, i])
        for q, (j, l) in enumerate(PAIRS):
            t = s[j] + s[l]

            def pick(fn):
                ii = fn(0.264, 4.28 * 4.28)
                mixed = fn(0.347, 4.28 * 4.0)
                gg = fn(0.43, 16.0)
                return jnp.where(t < 0.5, ii, jnp.where(t < 1.5, mixed, gg)).astype(f32)

            ka[q, z, i] = pick(lambda b, ll: 0.375 * b / ll)
            ka[6 + q, z, i] = pick(lambda b, ll: 0.125 * b)
            if W <= i < W + 4:
                kl[q, z, i - W] = pick(lambda b, ll: ll / 3.0)


def gradient(pos, emit, pieces, cells, e_row, refs, unroll=1):
    bs, fs, rs, kc, ka, kl, acc = refs
    ia, ib = cells
    count = pieces[0][1] - pieces[0][0] + 1
    offsets = ((0, 0), (0, 0), (0, 1), (1, 0))
    counted = any(za < W + CZ and zb >= W for za, zb in pieces)

    def bonds(z, i, which):
        found = {}
        cat = [pos(m, z, i) for m in range(3)]
        lo, hi = [c - H for c in cat], [c + H for c in cat]
        for j in which:
            dz, di = offsets[j]
            b = []
            for m in range(3):
                a = pos(3 + m, z - dz, i - di)
                if j == 1:
                    a = x_before(a)
                b.append(a - (lo[m] if SIGNS[j][m] > 0 else hi[m]))
            found[j] = b
        return found

    def keep(k, i, b, which):
        for j in which:
            for m in range(3):
                bs[3 * j + m, k, i] = x_after(b[j][m]) if j == 1 else b[j][m]

    def cation(z, i, which, energy):
        b = bonds(z, i, range(4))
        kd, md, kb, mb = (kc[n, z, i] for n in range(4))
        e = {}
        for j in range(4):
            for l in range(j, 4):
                if j not in which and l not in which:
                    continue
                d = dot(b[j], b[l])
                e[j, l] = e[l, j] = kd * d + md if j == l else kb * d + mb
        f = {j: [sum(e[j, l] * b[l][m] for l in range(4)) for m in range(3)] for j in which}
        total = None
        if energy:
            diag = sum(e[j, j] * e[j, j] for j in range(4))
            off = sum(e[p] * e[p] for p in PAIRS)
            total = diag * kc[4, z, i] + off * kc[5, z, i]
        return b, f, total

    def keep_forces(k, i, f):
        for j in f:
            for m in range(3):
                fs[3 * j + m, k, i] = f[j][m]

    def anion(z, k, i, which, energy):
        b = [[bs[3 * j + m, k + offsets[j][0], i + offsets[j][1]] for m in range(3)] for j in range(4)]
        c, total = {}, None
        for q, (j, l) in enumerate(PAIRS):
            if j not in which and l not in which:
                continue
            d = dot(b[j], b[l])
            c[j, l] = c[l, j] = ka[q, z, i] * d + ka[6 + q, z, i]
            if energy:
                part = c[j, l] * (d + kl[q, z, i - W])
                total = part if total is None else total + part
        r = {j: [sum(c[j, l] * b[l][m] for l in range(4) if l != j) for m in range(3)] for j in which}
        return r, total

    def tally(totals, scale):
        if counted:
            for z, total in totals:
                inside = jnp.logical_and(z >= W, z < W + CZ)
                acc[e_row] += jnp.where(inside, scale * total, 0.0)

    runs = [(za, zb, n * (count + 2)) for n, (za, zb) in enumerate(pieces)]

    def bond_plane(q):
        totals = []
        for za, zb, base in runs:
            z, k = za + q, base + 1 + q
            keep(k, ia - 1, bonds(z, ia - 1, (0, 1, 3)), (0, 1, 3))
            total = 0.0
            for i in range(ia, ib + 1):
                b, f, e = cation(z, i, range(4), counted and W <= i < W + 4)
                keep(k, i, b, range(4))
                keep_forces(k, i, f)
                if e is not None:
                    total = total + e
            b, f, _ = cation(z, ib + 1, (2,), False)
            keep(k, ib + 1, b, (2,))
            keep_forces(k, ib + 1, f)
            totals.append((z, total))
        tally(totals, 1.0)

    loop(count, bond_plane, unroll)

    for za, zb, base in runs:
        last = base + count + 1
        keep(last, ia - 1, bonds(zb + 1, ia - 1, (3,)), (3,))
        for i in range(ia, ib + 1):
            b, f, _ = cation(zb + 1, i, (3,), False)
            keep(last, i, b, (3,))
            keep_forces(last, i, f)
        for i in range(ia, ib + 2):
            which = ((0, 1) if i <= ib else ()) + ((2,) if i > ia else ())
            keep(base, i, bonds(za - 1, i, which), which)
    for za, zb, base in runs:
        for i in range(ia, ib + 1):
            r, _ = anion(za - 1, base, i, (3,), False)
            for m in range(3):
                rs[m, base, i] = r[3][m]

    def anion_plane(q):
        totals = []
        for za, zb, base in runs:
            z, k = za + q, base + 1 + q
            r, _ = anion(z, k, ia - 1, (2,), False)
            before = r[2]
            total = 0.0
            for i in range(ia, ib + 1):
                r, e = anion(z, k, i, range(4), counted and W <= i < W + 4)
                for m in range(3):
                    rs[m, k, i] = r[3][m]
                    f = [fs[3 * j + m, k, i] for j in range(4)]
                    back = r[0][m] + x_before(r[1][m]) + before[m] + rs[m, k - 1, i]
                    emit(m, z, i, -((f[0] + f[1]) + (f[2] + f[3]) + back))
                    ahead = f[0] + x_after(f[1]) + fs[6 + m, k, i + 1] + fs[9 + m, k + 1, i]
                    emit(3 + m, z, i, ahead + ((r[0][m] + r[1][m]) + (r[2][m] + r[3][m])))
                before = r[2]
                if e is not None:
                    total = total + e
            totals.append((z, total))
        tally(totals, 0.5)

    loop(count, anion_plane, unroll)


def advance(steps, state, scratch, p0, p1, p2, unroll):
    field, g0, pos1, g1, pos2, gs, kc, ka, kl, acc = state
    refs = (*scratch[:3], kc, ka, kl, acc)
    s0, s1 = steps[0], steps[1]

    def emit0(m, z, i, v):
        g0[m, z, i] = v
        pos1[m, z, i] = field[m, z, i] - s0 * v

    gradient(lambda m, z, i: field[m, z, i], emit0, p0, (1, IE - 2), E0, refs, unroll[0])

    def emit1(m, z, i, v):
        g1[m, z - 2, i - 2] = v
        mid, w = pos1[m, z, i] - s1 * v, s1 * g0[m, z, i]
        pos2[0, m, z - 2, i - 2] = mid + w
        pos2[1, m, z - 2, i - 2] = mid
        pos2[2, m, z - 2, i - 2] = mid - w
        pos2[3, m, z - 2, i - 2] = (mid - w) - w

    gradient(lambda m, z, i: pos1[m, z, i], emit1, p1, (2, IE - 3), E1, refs, unroll[1])

    def sample(k, carry):
        def emit2(m, z, i, v):
            gs[k, m, z - W, i - W] = v

        gradient(lambda m, z, i: pos2[k, m, z - 2, i - 2], emit2, p2, (W, W + 3), ES + k, refs, unroll[2])
        return carry

    lax.fori_loop(0, 4, sample, 0)

    def products(q):
        part = [None] * SUMS

        def add(n, v):
            part[n] = v if part[n] is None else part[n] + v

        for za, zb in p2:
            z = za + q
            for i in range(W, W + 4):
                for ch in range(6):
                    a, b = g0[ch, z, i], g1[ch, z - 2, i - 2]
                    g = [gs[k, ch, z - W, i - W] for k in range(4)]
                    add(N0, a * a)
                    add(N1, b * b)
                    add(X1, a * b)
                    for k in range(4):
                        add(GG1 + k, g[k] * b)
                        add(GG0 + k, g[k] * a)
                    for n, (k, l) in enumerate(GPAIRS):
                        add(GG + n, g[k] * g[l])
        for n, v in enumerate(part):
            if v is not None:
                acc[n] += v

    loop(p2[0][1] - p2[0][0] + 1, products)


def stage_inner(own0, own1, ylo, yhi, steps, *refs):
    state, scratch = refs[:STATE], refs[STATE:]
    field, kc, ka, kl, acc = state[0], *state[-4:]
    own = (own0, own1)
    acc[...] = jnp.zeros_like(acc)

    def fill(z):
        def natural(ch, h, at):
            return own[h][pl.ds((ch * CZ + z) * CY, CY), :]

        fill_plane(field, scratch[3:5], W + z, natural, lambda r, at: y_halo(ylo, yhi, r, z, at))

    loop(CZ, fill)
    loop(CZ, lambda z: cation_constants(field, kc, W + z))
    loop(CZ - 1, lambda z: anion_constants(field, ka, kl, W + z))
    top = W + CZ - 1
    advance(steps, state, scratch, [(W + 1, top - 1)], [(W + 2, top - 2)], [(W + 3, top - 3)], (2, 2, 2))


def stage_near(below, above, steps, *refs):
    state, scratch = refs[STATE : 2 * STATE], refs[2 * STATE :]
    field, kc, ka, kl = state[0], *state[-4:-1]
    top = W + CZ - 1

    def fill(k):
        fill_block(field, scratch[3:5], below, k, W - 2 + k)
        fill_block(field, scratch[3:5], above, k, top + 1 + k)

    loop(2, fill)
    for z in (W - 2, W - 1, top + 1, top + 2):
        cation_constants(field, kc, z)
    for z in (W - 2, W - 1, top, top + 1):
        anion_constants(field, ka, kl, z)
    advance(
        steps,
        state,
        scratch,
        [(W - 1, W), (top, top + 1)],
        [(W, W + 1), (top - 1, top)],
        [(W + 1, W + 2), (top - 2, top - 1)],
        (1, 1, 1),
    )


def stage_far(below, above, steps, *refs):
    state, sums, scratch = refs[STATE : 2 * STATE], refs[2 * STATE], refs[2 * STATE + 1 :]
    field, kc, ka, kl, acc = state[0], *state[-4:]
    top = W + CZ - 1
    fill_block(field, scratch[3:5], below, 0, 0)
    fill_block(field, scratch[3:5], above, 0, top + 3)
    cation_constants(field, kc, top + 3)
    for z in (0, top + 2):
        anion_constants(field, ka, kl, z)
    advance(
        steps,
        state,
        scratch,
        [(W - 2, W - 2), (top + 2, top + 2)],
        [(W - 1, W - 1), (top + 1, top + 1)],
        [(W, W), (top, top)],
        (1, 1, 1),
    )
    partial = jnp.sum(acc[...], axis=1)
    row = lax.broadcasted_iota(jnp.int32, (SUMS, 128), 0)
    lane = lax.broadcasted_iota(jnp.int32, (SUMS, 128), 1)
    spread = jnp.where(row == lane, jnp.sum(partial, axis=1, keepdims=True), 0.0)
    sums[...] = jnp.broadcast_to(jnp.sum(spread, axis=0, keepdims=True), sums.shape)


def finish(cell_count, gathered, steps, g0, pos1, g1, gs, out, energies, rows0, rows1):
    total = jnp.sum(gathered[...], axis=0, keepdims=True)

    def pick(n):
        return total[:, n : n + 1]

    t = (pick(N1) - pick(X1)) / (pick(N0) + 1e-06)
    lag = (
        -t * (t - 1.0) * (t - 2.0) * (1.0 / 6.0),
        (t + 1.0) * (t - 1.0) * (t - 2.0) * 0.5,
        -(t + 1.0) * t * (t - 2.0) * 0.5,
        (t + 1.0) * t * (t - 1.0) * (1.0 / 6.0),
    )
    t2, t3, t4 = t * t, t * t * t, t * t * t * t
    area = (
        -(t4 * 0.25 - t3 + t2) * (1.0 / 6.0),
        (t4 * 0.25 - t3 * (2.0 / 3.0) - t2 * 0.5 + 2.0 * t) * 0.5,
        -(t4 * 0.25 - t3 * (1.0 / 3.0) - t2) * 0.5,
        (t4 * 0.25 - t2 * 0.5) * (1.0 / 6.0),
    )
    norm2 = sum((1.0 if k == l else 2.0) * lag[k] * lag[l] * pick(GG + n) for n, (k, l) in enumerate(GPAIRS))
    cross2 = sum(lag[k] * pick(GG1 + k) for k in range(4))
    ratio = (norm2 - cross2) / (pick(N1) + 1e-06)
    s1, s2 = steps[1], steps[2]
    energy2 = pick(ES + 1) - s1 * sum(area[k] * pick(GG0 + k) for k in range(4))
    scale = 1.0 / cell_count
    energies[0] = jnp.sum(pick(E0)) * scale
    energies[1] = jnp.sum(pick(E1)) * scale
    energies[2] = jnp.sum(energy2) * scale
    along = s1 + s2 * ratio
    weights = [jnp.broadcast_to(w, (8, 128)) for w in [s2 * q for q in lag] + [along * t, along]]

    def plane(z):
        for ch in range(6):
            for i in range(4):
                parts = [gs[k, ch, z, i] for k in range(4)]
                parts += [g0[ch, z + W, i + W], g1[ch, z + 1, i + 1]]
                v = pos1[ch, z + W, i + W]
                for weight, part in zip(weights, parts):
                    v = v - weight * part
                rows0[pl.ds(ch * CY + i, 4, stride=4), :] = v[0:4]
                rows1[pl.ds(ch * CY + i, 4, stride=4), :] = v[4:8]
        for ch in range(6):
            for h, at in halves():
                rows = (rows0, rows1)[h]
                out[pl.ds(ch * CZ * CY + z * CY, CY), at] = rows[ch * CY : (ch + 1) * CY, :]

    loop(CZ, plane)


def vmem():
    return pl.BlockSpec(memory_space=pltpu.VMEM)


def smem():
    return pl.BlockSpec(memory_space=pltpu.SMEM)


def params(mib):
    return pltpu.CompilerParams(vmem_limit_bytes=mib * MIB)


def ring(value, axis, step):
    n = lax.axis_size(axis)
    return lax.ppermute(value, axis, [(i, (i + step) % n) for i in range(n)])


def per_device(displacement, species, step_sizes):
    shape = jax.ShapeDtypeStruct
    devices = lax.axis_size("slab") * lax.axis_size("col")
    cell_count = devices * CZ * CY * NX
    disp = displacement.reshape(6 * CZ * CY, NX)
    spec = species.reshape(CZ * CY, NX)
    edge = shape((W * CZ * 8, NX), f32)
    blocks = tuple(shape((len(planes) * PLANE, NX), f32) for planes in BLOCKS)
    half = shape((8 * CZ * CY, 128), f32)
    yup, ydown, *packed = pl.pallas_call(
        pack,
        out_shape=(edge, edge, *blocks, half, half),
        in_specs=[vmem()] * 2,
        out_specs=[vmem()] * (4 + len(blocks)),
        compiler_params=params(4),
        name="pack",
    )(disp, spec)
    own = packed[-2:]
    ylo, yhi = ring(yup, "col", 1), ring(ydown, "col", -1)
    up, down, far_up, far_down = pl.pallas_call(
        pack_halo,
        out_shape=blocks,
        in_specs=[vmem()] * (2 + len(blocks)),
        out_specs=[vmem()] * len(blocks),
        input_output_aliases={2 + n: n for n in range(len(blocks))},
        compiler_params=params(4),
        name="pack_halo",
    )(ylo, yhi, *packed[: len(blocks)])

    below, above = ring(up, "slab", 1), ring(down, "slab", -1)
    far_below, far_above = ring(far_up, "slab", 1), ring(far_down, "slab", -1)

    def tiles(*lead):
        return (*lead, 8, 128)

    state_shapes = tuple(
        shape(tiles(*lead), f32)
        for lead in (
            (7, ZE, IE),
            (6, ZE, IE),
            (6, ZE, IE),
            (6, ZE - 4, IE - 4),
            (4, 6, ZE - 4, IE - 4),
            (4, 6, CZ, 4),
            (6, ZE, IE),
            (12, ZE, IE),
            (6, ZE, 4),
            (SUMS,),
        )
    )
    scratch = [
        pltpu.VMEM(tiles(12, CZ, IE), f32),
        pltpu.VMEM(tiles(12, CZ, IE), f32),
        pltpu.VMEM(tiles(3, CZ, IE), f32),
        pltpu.VMEM((8 * 32, 128), f32),
        pltpu.VMEM((8 * 32, 128), f32),
    ]
    state = pl.pallas_call(
        stage_inner,
        out_shape=state_shapes,
        in_specs=[vmem()] * 4 + [smem()],
        out_specs=[vmem()] * STATE,
        scratch_shapes=scratch,
        compiler_params=params(14),
        cost_estimate=pl.CostEstimate(flops=100000000, bytes_accessed=1000000, transcendentals=0),
        name="stage_inner",
    )(*own, ylo, yhi, step_sizes)
    aliases = {3 + n: n for n in range(STATE)}
    state = pl.pallas_call(
        stage_near,
        out_shape=state_shapes,
        in_specs=[vmem()] * 2 + [smem()] + [vmem()] * STATE,
        out_specs=[vmem()] * STATE,
        scratch_shapes=scratch,
        input_output_aliases=aliases,
        compiler_params=params(14),
        cost_estimate=pl.CostEstimate(flops=100000000, bytes_accessed=1000000, transcendentals=0),
        name="stage_near",
    )(below, above, step_sizes, *state)
    *state, sums = pl.pallas_call(
        stage_far,
        out_shape=(*state_shapes, shape((devices, 128), f32)),
        in_specs=[vmem()] * 2 + [smem()] + [vmem()] * STATE,
        out_specs=[vmem()] * (STATE + 1),
        scratch_shapes=scratch,
        input_output_aliases=aliases,
        compiler_params=params(14),
        name="stage_far",
    )(far_below, far_above, step_sizes, *state)
    gathered = lax.all_to_all(sums.reshape(devices, 1, 128), ("slab", "col"), 0, 0)
    relaxed, energies = pl.pallas_call(
        functools.partial(finish, cell_count),
        out_shape=(shape((6 * CZ * CY, NX), f32), shape((3,), f32)),
        in_specs=[vmem(), smem()] + [vmem()] * 4,
        out_specs=[vmem(), smem()],
        scratch_shapes=[pltpu.VMEM((6 * CY, 128), f32)] * 2,
        compiler_params=params(4),
        name="finish",
    )(gathered.reshape(devices, 128), step_sizes, *state[1:4], state[5])
    return relaxed.reshape(displacement.shape), energies


def solution(mesh):
    in_specs = (P(None, "slab", "col", None), P("slab", "col", None), P())
    out_specs = (P(None, "slab", "col", None), P())
    return jax.shard_map(
        per_device, mesh=mesh, in_specs=in_specs, out_specs=out_specs, check_vma=False
    )
```

```python
import functools

import jax
import jax.numpy as jnp
from jax import lax
from jax.experimental import pallas as pl
from jax.experimental.pallas import tpu as pltpu
from jax.sharding import PartitionSpec as P

CZ, CY, NX = 8, 16, 256
W = 3
ZE = CZ + 2 * W
IE = 4 + 2 * W
ROWS = (-3, -2, -1, 16, 17, 18)
PLANE = 7 * CY + 6 * 8
H = 4.0 / 3.0**0.5
SIGNS = ((1, 1, 1), (1, -1, -1), (-1, 1, -1), (-1, -1, 1))
PAIRS = ((0, 1), (0, 2), (0, 3), (1, 2), (1, 3), (2, 3))
SAMPLES = (-1.0, 0.0, 1.0, 2.0)
E0, E1, ES, N0, N1, X1, GG1, GG0, GG = 0, 1, 2, 6, 7, 8, 9, 13, 17
GPAIRS = tuple((k, l) for k in range(4) for l in range(k, 4))
SUMS = 32
BLOCKS = ((6, 7), (0, 1), (5,), (2,))
MIB = 1024 * 1024
STATE = 11
f32 = jnp.float32


def halves():
    return (0, slice(0, 128)), (1, slice(128, NX))


def pack(disp, spec, yup, ydown, *outs):
    blocks, own = outs[:-2], outs[-2:]
    for h, at in halves():
        rows = own[h]
        rows[0 : 6 * CZ * CY, :] = disp[:, at]
        rows[6 * CZ * CY : 7 * CZ * CY, :] = spec[:, at].astype(f32)
        rows[7 * CZ * CY :, :] = jnp.zeros((CZ * CY, 128), f32)
        for dst, first in ((yup, CY - W), (ydown, 0)):
            for r in range(W):
                for z in range(CZ):
                    to = (r * CZ + z) * 8
                    dst[to : to + 8, at] = rows[pl.ds(z * CY + first + r, 8, stride=CZ * CY), :]
    for dst, planes in zip(blocks, BLOCKS):
        for k, z in enumerate(planes):
            for ch in range(7):
                to = k * PLANE + ch * CY
                for h, at in halves():
                    first = (ch * CZ + z) * CY
                    dst[to : to + CY, at] = own[h][first : first + CY, :]


def y_halo(ylo, yhi, r, z, at=slice(None)):
    src = ylo if r < W else yhi
    return src[pl.ds((r % W) * CZ * 8 + z * 8, 8), at]


def pack_halo(ylo, yhi, *refs):
    for dst, planes in zip(refs[len(BLOCKS) :], BLOCKS):
        for k, z in enumerate(planes):
            for r in range(6):
                to = k * PLANE + 7 * CY + r * 8
                dst[to : to + 8, :] = y_halo(ylo, yhi, r, z)


def lanes():
    return lax.broadcasted_iota(jnp.int32, (8, 128), 1)


def x_before(v):
    r = pltpu.roll(v, 1, 1)
    return jnp.where(lanes() == 0, pltpu.roll(r, 4, 0), r)


def x_after(v):
    r = pltpu.roll(v, 127, 1)
    return jnp.where(lanes() == 127, pltpu.roll(r, 4, 0), r)


def dot(a, b):
    return a[0] * b[0] + a[1] * b[1] + a[2] * b[2]


def loop(n, body, unroll=1):
    def step(k, carry):
        for q in range(unroll):
            body(k * unroll + q)
        return carry

    full = n // unroll
    if full > 1:
        lax.fori_loop(0, full, step, 0)
    else:
        full = 0
    for q in range(full * unroll, n):
        body(q)


def fill_plane(field, both, z, natural, halo):
    for h, at in halves():
        rows = both[h]
        for ch in range(7):
            rows[ch * 32 + 8 : ch * 32 + 24, :] = natural(ch, h, at)
        for r, y in enumerate(ROWS):
            rows[pl.ds(y + 8, 8, stride=32), :] = halo(r, at)
        for ch in range(7):
            for i in range(IE):
                first = ch * 32 + 8 - W + i
                field[ch, z, i, 4 * h : 4 * h + 4, :] = rows[pl.ds(first, 4, stride=4), :]


def fill_block(field, both, src, k, z):
    base = k * PLANE
    fill_plane(
        field,
        both,
        z,
        lambda ch, h, at: src[pl.ds(base + ch * CY, CY), at],
        lambda r, at: src[pl.ds(base + 7 * CY + r * 8, 8), at],
    )


def cation_constants(field, kc, z):
    for i in range(1, IE):
        indium = field[6, z, i] < 0.5

        def pick(fn):
            return jnp.where(indium, fn(0.848, 0.132, 4.28), fn(1.0, 0.215, 4.0)).astype(f32)

        kc[0, z, i] = pick(lambda a, b, l: 0.75 * a / l**2)
        kc[1, z, i] = pick(lambda a, b, l: -0.75 * a)
        kc[2, z, i] = pick(lambda a, b, l: 0.75 * b / l**2)
        kc[3, z, i] = pick(lambda a, b, l: 0.25 * b)
        kc[4, z, i] = pick(lambda a, b, l: l**2 / (3.0 * a))
        kc[5, z, i] = pick(lambda a, b, l: l**2 / (1.5 * b))


def anion_constants(field, ka, kl, z):
    for i in range(0, IE - 1):
        s = (field[6, z, i], x_after(field[6, z, i]), field[6, z, i + 1], field[6, z + 1, i])
        for q, (j, l) in enumerate(PAIRS):
            t = s[j] + s[l]

            def pick(fn):
                ii = fn(0.264, 4.28 * 4.28)
                mixed = fn(0.347, 4.28 * 4.0)
                gg = fn(0.43, 16.0)
                return jnp.where(t < 0.5, ii, jnp.where(t < 1.5, mixed, gg)).astype(f32)

            ka[q, z, i] = pick(lambda b, ll: 0.375 * b / ll)
            ka[6 + q, z, i] = pick(lambda b, ll: 0.125 * b)
            if W <= i < W + 4:
                kl[q, z, i - W] = pick(lambda b, ll: ll / 3.0)


OFFSETS = ((0, 0), (0, 0), (0, 1), (1, 0))


class Tiles:
    def __init__(self, ref, planes, cells):
        self.ref, self.planes, self.cells = ref, planes, cells

    def at(self, key):
        n, k, i = key
        return (n * self.planes + k) * self.cells + i

    def __getitem__(self, key):
        return self.ref[self.at(key)]

    def __setitem__(self, key, value):
        self.ref[self.at(key)] = value


def bonds(pos, z, i, which, h):
    found = {}
    cat = [pos(m, z, i) for m in range(3)]
    lo, hi = (cat, cat) if h == 0 else ([c - h for c in cat], [c + h for c in cat])
    for j in which:
        dz, di = OFFSETS[j]
        b = []
        for m in range(3):
            a = pos(3 + m, z - dz, i - di)
            if j == 1:
                a = x_before(a)
            b.append(a - (lo[m] if SIGNS[j][m] > 0 else hi[m]))
        found[j] = b
    return found


def cation_terms(b, k, which, energy):
    e = {}
    for j in range(4):
        for l in range(j, 4):
            if j not in which and l not in which:
                continue
            d = dot(b[j], b[l])
            e[j, l] = e[l, j] = k[0] * d + k[1] if j == l else k[2] * d + k[3]
    f = {j: [sum(e[j, l] * b[l][m] for l in range(4)) for m in range(3)] for j in which}
    total = None
    if energy:
        diag = sum(e[j, j] * e[j, j] for j in range(4))
        off = sum(e[p] * e[p] for p in PAIRS)
        total = diag * k[4] + off * k[5]
    return f, total


def anion_terms(b, k, lengths, which):
    c, total = {}, None
    for q, (j, l) in enumerate(PAIRS):
        if j not in which and l not in which:
            continue
        d = dot(b[j], b[l])
        c[j, l] = c[l, j] = k[q] * d + k[6 + q]
        if lengths is not None:
            part = c[j, l] * (d + lengths[q])
            total = part if total is None else total + part
    r = {j: [sum(c[j, l] * b[l][m] for l in range(4) if l != j) for m in range(3)] for j in which}
    return r, total


def sampled(pos, step, emit, pieces, refs):
    bs, ds, fs, rs, kc, ka, kl, acc = refs
    ia, ib = W, W + 3
    count = pieces[0][1] - pieces[0][0] + 1
    stride = pieces[-1][0] - pieces[0][0]
    four = range(4)

    def here(z, i, which):
        b = bonds(lambda m, z, i: pos[m, z - 2, i - 2], z, i, which, H)
        d = bonds(lambda m, z, i: step[m, z - 2, i - 2], z, i, which, 0)
        return b, d

    def keep(k, i, b, d, which):
        for j in which:
            for m in range(3):
                for dst, v in ((bs, b[j][m]), (ds, d[j][m])):
                    dst[3 * j + m, k, i - 2] = x_after(v) if j == 1 else v

    def onward(b, d):
        return {j: [b[j][m] + d[j][m] for m in range(3)] for j in b}

    def cation(z, k, i, which, kept, energy):
        b, d = here(z, i, four)
        keep(k, i, b, d, kept)
        consts = [kc[n, z, i] for n in range(6 if energy else 4)]
        total = None
        for n in four:
            f, e = cation_terms(b, consts, which, energy and n == 1)
            for j in which:
                for m in range(3):
                    fs[12 * n + 3 * j + m, k, i - 2] = f[j][m]
            total = e if e is not None else total
            b = onward(b, d)
        return total

    def anion(z, k, i, which, energy):
        b, d = (
            {j: [src[3 * j + m, k + OFFSETS[j][0], i + OFFSETS[j][1] - 2] for m in range(3)] for j in four}
            for src in (bs, ds)
        )
        need = [q for q, p in enumerate(PAIRS) if p[0] in which or p[1] in which]
        consts = {q + o: ka[q + o, z, i] for q in need for o in (0, 6)}
        lengths = [kl[q, z, i - W] for q in range(6)] if energy else None
        found, total = [], None
        for n in four:
            r, e = anion_terms(b, consts, lengths if n == 1 else None, which)
            found.append(r)
            total = e if e is not None else total
            b = onward(b, d)
        return found, total

    def piece(p):
        za = pieces[0][0] + p * stride
        zb = za + count - 1

        def bond_plane(q):
            z, k = za + q, 1 + q
            keep(k, ia - 1, *here(z, ia - 1, (0, 1, 3)), (0, 1, 3))
            total = 0.0
            for i in range(ia, ib + 1):
                total = total + cation(z, k, i, four, four, True)
            cation(z, k, ib + 1, (2,), (2,), False)
            acc[ES + 1] += total

        loop(count, bond_plane)
        last = count + 1
        keep(last, ia - 1, *here(zb + 1, ia - 1, (3,)), (3,))
        for i in range(ia, ib + 1):
            cation(zb + 1, last, i, (3,), (3,), False)
        for i in range(ia, ib + 2):
            which = ((0, 1) if i <= ib else ()) + ((2,) if i > ia else ())
            keep(0, i, *here(za - 1, i, which), which)
        for i in range(ia, ib + 1):
            found, _ = anion(za - 1, 0, i, (3,), False)
            for n in four:
                for m in range(3):
                    rs[3 * n + m, 0, i - 2] = found[n][3][m]

        def anion_plane(q):
            z, k = za + q, 1 + q
            found, _ = anion(z, k, ia - 1, (2,), False)
            before = [r[2] for r in found]
            total = 0.0
            for i in range(ia, ib + 1):
                found, e = anion(z, k, i, four, True)
                total = total + e
                for n, r in enumerate(found):
                    for m in range(3):
                        rs[3 * n + m, k, i - 2] = r[3][m]
                        f = [fs[12 * n + 3 * j + m, k, i - 2] for j in four]
                        back = r[0][m] + x_before(r[1][m]) + before[n][m] + rs[3 * n + m, k - 1, i - 2]
                        emit(n, m, z, i, -((f[0] + f[1]) + (f[2] + f[3]) + back))
                        ahead = f[0] + x_after(f[1]) + fs[12 * n + 6 + m, k, i - 1] + fs[12 * n + 9 + m, k + 1, i - 2]
                        emit(n, 3 + m, z, i, ahead + ((r[0][m] + r[1][m]) + (r[2][m] + r[3][m])))
                before = [r[2] for r in found]
            acc[ES + 1] += 0.5 * total

        for q in range(count):
            anion_plane(q)

    loop(len(pieces), piece)


def gradient(pos, emit, pieces, cells, e_row, refs, unroll=1):
    bs, fs, rs, kc, ka, kl, acc = refs
    ia, ib = cells
    count = pieces[0][1] - pieces[0][0] + 1
    counted = any(za < W + CZ and zb >= W for za, zb in pieces)

    def here(z, i, which):
        return bonds(pos, z, i, which, H)

    def keep(k, i, b, which):
        for j in which:
            for m in range(3):
                bs[3 * j + m, k, i] = x_after(b[j][m]) if j == 1 else b[j][m]

    def cation(z, i, which, energy):
        b = here(z, i, range(4))
        f, total = cation_terms(b, [kc[n, z, i] for n in range(6 if energy else 4)], which, energy)
        return b, f, total

    def keep_forces(k, i, f):
        for j in f:
            for m in range(3):
                fs[3 * j + m, k, i] = f[j][m]

    def anion(z, k, i, which, energy):
        b = [[bs[3 * j + m, k + OFFSETS[j][0], i + OFFSETS[j][1]] for m in range(3)] for j in range(4)]
        need = [q for q, p in enumerate(PAIRS) if p[0] in which or p[1] in which]
        consts = {q + o: ka[q + o, z, i] for q in need for o in (0, 6)}
        lengths = [kl[q, z, i - W] for q in range(6)] if energy else None
        return anion_terms(b, consts, lengths, which)

    def tally(totals, scale):
        if counted:
            for z, total in totals:
                inside = jnp.logical_and(z >= W, z < W + CZ)
                acc[e_row] += jnp.where(inside, scale * total, 0.0)

    runs = [(za, zb, n * (count + 2)) for n, (za, zb) in enumerate(pieces)]

    def bond_plane(q):
        totals = []
        for za, zb, base in runs:
            z, k = za + q, base + 1 + q
            keep(k, ia - 1, here(z, ia - 1, (0, 1, 3)), (0, 1, 3))
            total = 0.0
            for i in range(ia, ib + 1):
                b, f, e = cation(z, i, range(4), counted and W <= i < W + 4)
                keep(k, i, b, range(4))
                keep_forces(k, i, f)
                if e is not None:
                    total = total + e
            b, f, _ = cation(z, ib + 1, (2,), False)
            keep(k, ib + 1, b, (2,))
            keep_forces(k, ib + 1, f)
            totals.append((z, total))
        tally(totals, 1.0)

    loop(count, bond_plane, unroll)

    for za, zb, base in runs:
        last = base + count + 1
        keep(last, ia - 1, here(zb + 1, ia - 1, (3,)), (3,))
        for i in range(ia, ib + 1):
            b, f, _ = cation(zb + 1, i, (3,), False)
            keep(last, i, b, (3,))
            keep_forces(last, i, f)
        for i in range(ia, ib + 2):
            which = ((0, 1) if i <= ib else ()) + ((2,) if i > ia else ())
            keep(base, i, here(za - 1, i, which), which)
    for za, zb, base in runs:
        for i in range(ia, ib + 1):
            r, _ = anion(za - 1, base, i, (3,), False)
            for m in range(3):
                rs[m, base, i] = r[3][m]

    def anion_plane(q):
        totals = []
        for za, zb, base in runs:
            z, k = za + q, base + 1 + q
            r, _ = anion(z, k, ia - 1, (2,), False)
            before = r[2]
            total = 0.0
            for i in range(ia, ib + 1):
                r, e = anion(z, k, i, range(4), counted and W <= i < W + 4)
                for m in range(3):
                    rs[m, k, i] = r[3][m]
                    f = [fs[3 * j + m, k, i] for j in range(4)]
                    back = r[0][m] + x_before(r[1][m]) + before[m] + rs[m, k - 1, i]
                    emit(m, z, i, -((f[0] + f[1]) + (f[2] + f[3]) + back))
                    ahead = f[0] + x_after(f[1]) + fs[6 + m, k, i + 1] + fs[9 + m, k + 1, i]
                    emit(3 + m, z, i, ahead + ((r[0][m] + r[1][m]) + (r[2][m] + r[3][m])))
                before = r[2]
                if e is not None:
                    total = total + e
            totals.append((z, total))
        tally(totals, 0.5)

    loop(count, anion_plane, unroll)


def advance(steps, state, scratch, p0, p1, p2, unroll):
    field, g0, pos1, g1, pos2, step, gs, kc, ka, kl, acc = state
    bs, fs, rs = (Tiles(ref, CZ, IE) for ref in scratch[:3])
    refs = (bs, fs, rs, kc, ka, kl, acc)
    s0, s1 = steps[0], steps[1]

    def emit0(m, z, i, v):
        g0[m, z, i] = v
        pos1[m, z, i] = field[m, z, i] - s0 * v

    gradient(lambda m, z, i: field[m, z, i], emit0, p0, (1, IE - 2), E0, refs, unroll[0])

    def emit1(m, z, i, v):
        g1[m, z - 2, i - 2] = v
        w = s1 * g0[m, z, i]
        pos2[m, z - 2, i - 2] = (pos1[m, z, i] - s1 * v) + w
        step[m, z - 2, i - 2] = -w

    gradient(lambda m, z, i: pos1[m, z, i], emit1, p1, (2, IE - 3), E1, refs, unroll[1])

    def emit2(k, m, z, i, v):
        gs[k, m, z - W, i - W] = v

    sampled(pos2, step, emit2, p2, (bs, scratch[5], Tiles(scratch[1], 4, 6), scratch[6], kc, ka, kl, acc))

    def products(q):
        part = [None] * SUMS

        def add(n, v):
            part[n] = v if part[n] is None else part[n] + v

        for za, zb in p2:
            z = za + q
            for i in range(W, W + 4):
                for ch in range(6):
                    a, b = g0[ch, z, i], g1[ch, z - 2, i - 2]
                    g = [gs[k, ch, z - W, i - W] for k in range(4)]
                    add(N0, a * a)
                    add(N1, b * b)
                    add(X1, a * b)
                    for k in range(4):
                        add(GG1 + k, g[k] * b)
                        add(GG0 + k, g[k] * a)
                    for n, (k, l) in enumerate(GPAIRS):
                        add(GG + n, g[k] * g[l])
        for n, v in enumerate(part):
            if v is not None:
                acc[n] += v

    loop(p2[0][1] - p2[0][0] + 1, products)


def stage_inner(own0, own1, ylo, yhi, steps, *refs):
    state, scratch = refs[:STATE], refs[STATE:]
    field, kc, ka, kl, acc = state[0], *state[-4:]
    own = (own0, own1)
    acc[...] = jnp.zeros_like(acc)

    def fill(z):
        def natural(ch, h, at):
            return own[h][pl.ds((ch * CZ + z) * CY, CY), :]

        fill_plane(field, scratch[3:5], W + z, natural, lambda r, at: y_halo(ylo, yhi, r, z, at))

    loop(CZ, fill)
    loop(CZ, lambda z: cation_constants(field, kc, W + z))
    loop(CZ - 1, lambda z: anion_constants(field, ka, kl, W + z))
    top = W + CZ - 1
    advance(steps, state, scratch, [(W + 1, top - 1)], [(W + 2, top - 2)], [(W + 3, top - 3)], (2, 2, 2))


def stage_near(below, above, steps, *refs):
    state, scratch = refs[STATE : 2 * STATE], refs[2 * STATE :]
    field, kc, ka, kl = state[0], *state[-4:-1]
    top = W + CZ - 1

    def fill(k):
        fill_block(field, scratch[3:5], below, k, W - 2 + k)
        fill_block(field, scratch[3:5], above, k, top + 1 + k)

    loop(2, fill)
    for z in (W - 2, W - 1, top + 1, top + 2):
        cation_constants(field, kc, z)
    for z in (W - 2, W - 1, top, top + 1):
        anion_constants(field, ka, kl, z)
    advance(
        steps,
        state,
        scratch,
        [(W - 1, W), (top, top + 1)],
        [(W, W + 1), (top - 1, top)],
        [(W + 1, W + 2), (top - 2, top - 1)],
        (1, 1, 1),
    )


def stage_far(below, above, steps, *refs):
    state, sums, scratch = refs[STATE : 2 * STATE], refs[2 * STATE], refs[2 * STATE + 1 :]
    field, kc, ka, kl, acc = state[0], *state[-4:]
    top = W + CZ - 1
    fill_block(field, scratch[3:5], below, 0, 0)
    fill_block(field, scratch[3:5], above, 0, top + 3)
    cation_constants(field, kc, top + 3)
    for z in (0, top + 2):
        anion_constants(field, ka, kl, z)
    advance(
        steps,
        state,
        scratch,
        [(W - 2, W - 2), (top + 2, top + 2)],
        [(W - 1, W - 1), (top + 1, top + 1)],
        [(W, W), (top, top)],
        (1, 1, 1),
    )
    partial = jnp.sum(acc[...], axis=1)
    row = lax.broadcasted_iota(jnp.int32, (SUMS, 128), 0)
    lane = lax.broadcasted_iota(jnp.int32, (SUMS, 128), 1)
    spread = jnp.where(row == lane, jnp.sum(partial, axis=1, keepdims=True), 0.0)
    sums[...] = jnp.broadcast_to(jnp.sum(spread, axis=0, keepdims=True), sums.shape)


def finish(cell_count, gathered, steps, g0, pos1, g1, gs, out, energies, rows0, rows1):
    total = jnp.sum(gathered[...], axis=0, keepdims=True)

    def pick(n):
        return total[:, n : n + 1]

    t = (pick(N1) - pick(X1)) / (pick(N0) + 1e-06)
    lag = (
        -t * (t - 1.0) * (t - 2.0) * (1.0 / 6.0),
        (t + 1.0) * (t - 1.0) * (t - 2.0) * 0.5,
        -(t + 1.0) * t * (t - 2.0) * 0.5,
        (t + 1.0) * t * (t - 1.0) * (1.0 / 6.0),
    )
    t2, t3, t4 = t * t, t * t * t, t * t * t * t
    area = (
        -(t4 * 0.25 - t3 + t2) * (1.0 / 6.0),
        (t4 * 0.25 - t3 * (2.0 / 3.0) - t2 * 0.5 + 2.0 * t) * 0.5,
        -(t4 * 0.25 - t3 * (1.0 / 3.0) - t2) * 0.5,
        (t4 * 0.25 - t2 * 0.5) * (1.0 / 6.0),
    )
    norm2 = sum((1.0 if k == l else 2.0) * lag[k] * lag[l] * pick(GG + n) for n, (k, l) in enumerate(GPAIRS))
    cross2 = sum(lag[k] * pick(GG1 + k) for k in range(4))
    ratio = (norm2 - cross2) / (pick(N1) + 1e-06)
    s1, s2 = steps[1], steps[2]
    energy2 = pick(ES + 1) - s1 * sum(area[k] * pick(GG0 + k) for k in range(4))
    scale = 1.0 / cell_count
    energies[0] = jnp.sum(pick(E0)) * scale
    energies[1] = jnp.sum(pick(E1)) * scale
    energies[2] = jnp.sum(energy2) * scale
    along = s1 + s2 * ratio
    weights = [jnp.broadcast_to(w, (8, 128)) for w in [s2 * q for q in lag] + [along * t, along]]

    def plane(z):
        for ch in range(6):
            for i in range(4):
                parts = [gs[k, ch, z, i] for k in range(4)]
                parts += [g0[ch, z + W, i + W], g1[ch, z + 1, i + 1]]
                v = pos1[ch, z + W, i + W]
                for weight, part in zip(weights, parts):
                    v = v - weight * part
                rows0[pl.ds(ch * CY + i, 4, stride=4), :] = v[0:4]
                rows1[pl.ds(ch * CY + i, 4, stride=4), :] = v[4:8]
        for ch in range(6):
            for h, at in halves():
                rows = (rows0, rows1)[h]
                out[pl.ds(ch * CZ * CY + z * CY, CY), at] = rows[ch * CY : (ch + 1) * CY, :]

    loop(CZ, plane)


def vmem():
    return pl.BlockSpec(memory_space=pltpu.VMEM)


def smem():
    return pl.BlockSpec(memory_space=pltpu.SMEM)


def params(mib):
    return pltpu.CompilerParams(vmem_limit_bytes=mib * MIB)


def ring(value, axis, step):
    n = lax.axis_size(axis)
    return lax.ppermute(value, axis, [(i, (i + step) % n) for i in range(n)])


def per_device(displacement, species, step_sizes):
    shape = jax.ShapeDtypeStruct
    devices = lax.axis_size("slab") * lax.axis_size("col")
    cell_count = devices * CZ * CY * NX
    disp = displacement.reshape(6 * CZ * CY, NX)
    spec = species.reshape(CZ * CY, NX)
    edge = shape((W * CZ * 8, NX), f32)
    blocks = tuple(shape((len(planes) * PLANE, NX), f32) for planes in BLOCKS)
    half = shape((8 * CZ * CY, 128), f32)
    yup, ydown, *packed = pl.pallas_call(
        pack,
        out_shape=(edge, edge, *blocks, half, half),
        in_specs=[vmem()] * 2,
        out_specs=[vmem()] * (4 + len(blocks)),
        compiler_params=params(4),
        name="pack",
    )(disp, spec)
    own = packed[-2:]
    ylo, yhi = ring(yup, "col", 1), ring(ydown, "col", -1)
    up, down, far_up, far_down = pl.pallas_call(
        pack_halo,
        out_shape=blocks,
        in_specs=[vmem()] * (2 + len(blocks)),
        out_specs=[vmem()] * len(blocks),
        input_output_aliases={2 + n: n for n in range(len(blocks))},
        compiler_params=params(4),
        name="pack_halo",
    )(ylo, yhi, *packed[: len(blocks)])

    below, above = ring(up, "slab", 1), ring(down, "slab", -1)

    def tiles(*lead):
        return (*lead, 8, 128)

    state_shapes = tuple(
        shape(tiles(*lead), f32)
        for lead in (
            (7, ZE, IE),
            (6, ZE, IE),
            (6, ZE, IE),
            (6, ZE - 4, IE - 4),
            (6, ZE - 4, IE - 4),
            (6, ZE - 4, IE - 4),
            (4, 6, CZ, 4),
            (6, ZE, IE),
            (12, ZE - 1, IE - 1),
            (6, ZE, 4),
            (SUMS,),
        )
    )
    scratch = [
        pltpu.VMEM(tiles(12 * CZ * IE), f32),
        pltpu.VMEM(tiles(48 * 4 * 6), f32),
        pltpu.VMEM(tiles(3 * CZ * IE), f32),
        pltpu.VMEM((8 * 32, 128), f32),
        pltpu.VMEM((8 * 32, 128), f32),
        pltpu.VMEM(tiles(12, 4, 6), f32),
        pltpu.VMEM(tiles(12, 4, 6), f32),
    ]
    state = pl.pallas_call(
        stage_inner,
        out_shape=state_shapes,
        in_specs=[vmem()] * 4 + [smem()],
        out_specs=[vmem()] * STATE,
        scratch_shapes=scratch,
        compiler_params=params(17),
        cost_estimate=pl.CostEstimate(flops=100000000, bytes_accessed=1000000, transcendentals=0),
        name="stage_inner",
    )(*own, ylo, yhi, step_sizes)
    state = list(state)
    far_up, far_down, state[-1] = lax.optimization_barrier((far_up, far_down, state[-1]))
    far_below, far_above = ring(far_up, "slab", 1), ring(far_down, "slab", -1)
    aliases = {3 + n: n for n in range(STATE)}
    state = pl.pallas_call(
        stage_near,
        out_shape=state_shapes,
        in_specs=[vmem()] * 2 + [smem()] + [vmem()] * STATE,
        out_specs=[vmem()] * STATE,
        scratch_shapes=scratch,
        input_output_aliases=aliases,
        compiler_params=params(17),
        cost_estimate=pl.CostEstimate(flops=100000000, bytes_accessed=1000000, transcendentals=0),
        name="stage_near",
    )(below, above, step_sizes, *state)
    *state, sums = pl.pallas_call(
        stage_far,
        out_shape=(*state_shapes, shape((devices, 128), f32)),
        in_specs=[vmem()] * 2 + [smem()] + [vmem()] * STATE,
        out_specs=[vmem()] * (STATE + 1),
        scratch_shapes=scratch,
        input_output_aliases=aliases,
        compiler_params=params(17),
        name="stage_far",
    )(far_below, far_above, step_sizes, *state)
    gathered = lax.all_to_all(sums.reshape(devices, 1, 128), ("slab", "col"), 0, 0)
    relaxed, energies = pl.pallas_call(
        functools.partial(finish, cell_count),
        out_shape=(shape((6 * CZ * CY, NX), f32), shape((3,), f32)),
        in_specs=[vmem(), smem()] + [vmem()] * 4,
        out_specs=[vmem(), smem()],
        scratch_shapes=[pltpu.VMEM((6 * CY, 128), f32)] * 2,
        compiler_params=params(4),
        name="finish",
    )(gathered.reshape(devices, 128), step_sizes, *state[1:4], state[6])
    return relaxed.reshape(displacement.shape), energies


def solution(mesh):
    in_specs = (P(None, "slab", "col", None), P("slab", "col", None), P())
    out_specs = (P(None, "slab", "col", None), P())
    return jax.shard_map(
        per_device, mesh=mesh, in_specs=in_specs, out_specs=out_specs, check_vma=False
    )
```

```python
import functools

import jax
import jax.numpy as jnp
from jax import lax
from jax.experimental import pallas as pl
from jax.experimental.pallas import tpu as pltpu
from jax.sharding import PartitionSpec as P

CZ, CY, NX = 8, 16, 256
W = 3
ZE = CZ + 2 * W
IE = 4 + 2 * W
ROWS = (-3, -2, -1, 16, 17, 18)
PLANE = 7 * CY + 6 * 8
H = 4.0 / 3.0**0.5
SIGNS = ((1, 1, 1), (1, -1, -1), (-1, 1, -1), (-1, -1, 1))
PAIRS = ((0, 1), (0, 2), (0, 3), (1, 2), (1, 3), (2, 3))
SAMPLES = (-1.0, 0.0, 1.0, 2.0)
E0, E1, ES, N0, N1, X1, GG1, GG0, GG = 0, 1, 2, 6, 7, 8, 9, 13, 17
GPAIRS = tuple((k, l) for k in range(4) for l in range(k, 4))
SUMS = 32
BLOCKS = ((7,), (0,), (6,), (1,), (5,), (2,))
MIB = 1024 * 1024
STATE = 17
f32 = jnp.float32


def halves():
    return (0, slice(0, 128)), (1, slice(128, NX))


def pack(disp_hbm, spec_hbm, yup, ydown, *refs):
    blocks, own = refs[: len(BLOCKS)], refs[len(BLOCKS) : len(BLOCKS) + 2]
    disp, spec, sems = refs[len(BLOCKS) + 2 :]
    copies = [
        pltpu.make_async_copy(src, dst, sems.at[n])
        for n, (src, dst) in enumerate(((disp_hbm, disp), (spec_hbm, spec)))
    ]
    for copy in copies:
        copy.start()
    for copy in copies:
        copy.wait()
    for h, at in halves():
        rows = own[h]
        rows[0 : 6 * CZ * CY, :] = disp[:, at]
        rows[6 * CZ * CY : 7 * CZ * CY, :] = spec[:, at].astype(f32)
        rows[7 * CZ * CY :, :] = jnp.zeros((CZ * CY, 128), f32)
        for dst, first in ((yup, CY - W), (ydown, 0)):
            for r in range(W):
                for z in range(CZ):
                    to = (r * CZ + z) * 8
                    dst[to : to + 8, at] = rows[pl.ds(z * CY + first + r, 8, stride=CZ * CY), :]
    for dst, planes in zip(blocks, BLOCKS):
        for k, z in enumerate(planes):
            for ch in range(7):
                to = k * PLANE + ch * CY
                for h, at in halves():
                    first = (ch * CZ + z) * CY
                    dst[to : to + CY, at] = own[h][first : first + CY, :]


def y_halo(ylo, yhi, r, z, at=slice(None)):
    src = ylo if r < W else yhi
    return src[pl.ds((r % W) * CZ * 8 + z * 8, 8), at]


def pack_halo(ylo, yhi, *refs):
    for dst, planes in zip(refs[len(BLOCKS) :], BLOCKS):
        for k, z in enumerate(planes):
            for r in range(6):
                to = k * PLANE + 7 * CY + r * 8
                dst[to : to + 8, :] = y_halo(ylo, yhi, r, z)


def lanes():
    return lax.broadcasted_iota(jnp.int32, (8, 128), 1)


def x_before(v):
    r = pltpu.roll(v, 1, 1)
    return jnp.where(lanes() == 0, pltpu.roll(r, 4, 0), r)


def x_after(v):
    r = pltpu.roll(v, 127, 1)
    return jnp.where(lanes() == 127, pltpu.roll(r, 4, 0), r)


def dot(a, b):
    return a[0] * b[0] + a[1] * b[1] + a[2] * b[2]


def loop(n, body, unroll=1):
    def step(k, carry):
        for q in range(unroll):
            body(k * unroll + q)
        return carry

    full = n // unroll
    if full > 1:
        lax.fori_loop(0, full, step, 0)
    else:
        full = 0
    for q in range(full * unroll, n):
        body(q)


def fill_plane(field, both, z, natural, halo):
    for h, at in halves():
        rows = both[h]
        for ch in range(7):
            rows[ch * 32 + 8 : ch * 32 + 24, :] = natural(ch, h, at)
        for r, y in enumerate(ROWS):
            rows[pl.ds(y + 8, 8, stride=32), :] = halo(r, at)
        for ch in range(7):
            for i in range(IE):
                first = ch * 32 + 8 - W + i
                v = rows[pl.ds(first, 4, stride=4), :]
                field[ch, z, i, 4 * h : 4 * h + 4, :] = v + H if 3 <= ch < 6 else v


def fill_block(field, both, src, k, z):
    base = k * PLANE
    fill_plane(
        field,
        both,
        z,
        lambda ch, h, at: src[pl.ds(base + ch * CY, CY), at],
        lambda r, at: src[pl.ds(base + 7 * CY + r * 8, 8), at],
    )


def cation_constants(field, kc, z):
    for i in range(1, IE):
        indium = field[6, z, i] < 0.5

        def pick(fn):
            return jnp.where(indium, fn(0.848, 0.132, 4.28), fn(1.0, 0.215, 4.0)).astype(f32)

        kc[0, z, i] = pick(lambda a, b, l: 0.75 * a / l**2)
        kc[1, z, i] = pick(lambda a, b, l: -0.75 * a)
        kc[2, z, i] = pick(lambda a, b, l: 0.75 * b / l**2)
        kc[3, z, i] = pick(lambda a, b, l: 0.25 * b)
        kc[4, z, i] = pick(lambda a, b, l: l**2 / (3.0 * a))
        kc[5, z, i] = pick(lambda a, b, l: l**2 / (1.5 * b))


def anion_constants(field, ka, kl, z):
    for i in range(0, IE - 1):
        s = (field[6, z, i], x_after(field[6, z, i]), field[6, z, i + 1], field[6, z + 1, i])
        for q, (j, l) in enumerate(PAIRS):
            t = s[j] + s[l]

            def pick(fn):
                ii = fn(0.264, 4.28 * 4.28)
                mixed = fn(0.347, 4.28 * 4.0)
                gg = fn(0.43, 16.0)
                return jnp.where(t < 0.5, ii, jnp.where(t < 1.5, mixed, gg)).astype(f32)

            ka[q, z, i] = pick(lambda b, ll: 0.375 * b / ll)
            ka[6 + q, z, i] = pick(lambda b, ll: 0.125 * b)
            if W <= i < W + 4:
                kl[q, z, i - W] = pick(lambda b, ll: ll / 3.0)


OFFSETS = ((0, 0), (0, 0), (0, 1), (1, 0))


class Tiles:
    def __init__(self, ref, planes, cells):
        self.ref, self.planes, self.cells = ref, planes, cells

    def at(self, key):
        n, k, i = key
        return (n * self.planes + k) * self.cells + i

    def __getitem__(self, key):
        return self.ref[self.at(key)]

    def __setitem__(self, key, value):
        self.ref[self.at(key)] = value


def bonds(pos, z, i, which, h):
    found = {}
    cat = [pos(m, z, i) for m in range(3)]
    lo, hi = cat, (cat if h == 0 else [c + 2.0 * h for c in cat])
    for j in which:
        dz, di = OFFSETS[j]
        b = []
        for m in range(3):
            a = pos(3 + m, z - dz, i - di)
            if j == 1:
                a = x_before(a)
            b.append(a - (lo[m] if SIGNS[j][m] > 0 else hi[m]))
        found[j] = b
    return found


def cation_terms(b, k, which, energy):
    e = {}
    for j in range(4):
        for l in range(j, 4):
            if j not in which and l not in which:
                continue
            d = dot(b[j], b[l])
            e[j, l] = e[l, j] = k[0] * d + k[1] if j == l else k[2] * d + k[3]
    f = {j: [sum(e[j, l] * b[l][m] for l in range(4)) for m in range(3)] for j in which}
    total = None
    if energy:
        diag = sum(e[j, j] * e[j, j] for j in range(4))
        off = sum(e[p] * e[p] for p in PAIRS)
        total = diag * k[4] + off * k[5]
    return f, total


def anion_terms(b, k, lengths, which):
    c, total = {}, None
    for q, (j, l) in enumerate(PAIRS):
        if j not in which and l not in which:
            continue
        d = dot(b[j], b[l])
        c[j, l] = c[l, j] = k[q] * d + k[6 + q]
        if lengths is not None:
            part = c[j, l] * (d + lengths[q])
            total = part if total is None else total + part
    r = {j: [sum(c[j, l] * b[l][m] for l in range(4) if l != j) for m in range(3)] for j in which}
    return r, total


class Kind:
    def __init__(self, pos, step, emit, cells, e_row, scratch, consts, acc, low, high):
        self.pos, self.step, self.emit, self.e_row = pos, step, emit, e_row
        self.ia, self.ib = cells
        self.kc, self.ka, self.kl = consts
        self.acc, self.low, self.high = acc, low, high
        self.four = range(1 if step is None else 4)
        self.count = len(self.four)
        planes = CZ if step is None else 4
        width = self.ib - self.ia + 3
        self.bs, self.ds, self.fs, self.rs = (Tiles(ref, planes, width) for ref in scratch)
        self.counted = 0 if step is None else 1

    def here(self, z, i, which):
        b = bonds(self.pos, z, i, which, H)
        return b, None if self.step is None else bonds(self.step, z, i, which, 0)

    def keep(self, k, i, both, which):
        c = i - self.ia + 1
        for dst, v in zip((self.bs, self.ds), both):
            if v is not None:
                for j in which:
                    for m in range(3):
                        dst[3 * j + m, k, c] = x_after(v[j][m]) if j == 1 else v[j][m]

    def kept(self, k, i):
        c = i - self.ia + 1
        both = [self.bs, self.ds] if self.step is not None else [self.bs]
        return [{j: [src[3 * j + m, k + OFFSETS[j][0], c + OFFSETS[j][1]] for m in range(3)] for j in range(4)} for src in both]

    def onward(self, both):
        b, d = both[0], both[1] if len(both) > 1 else None
        return b if d is None else {j: [b[j][m] + d[j][m] for m in range(3)] for j in b}

    def cation(self, z, i, which, energy):
        both = self.here(z, i, range(4))
        consts = [self.kc[n, z, i] for n in range(6 if energy else 4)]
        found, total, b = [], None, both[0]
        for n in self.four:
            f, e = cation_terms(b, consts, which, energy and n == self.counted)
            found.append(f)
            total = e if e is not None else total
            if n + 1 < self.count:
                b = self.onward((b, both[1]))
        return both, found, total

    def anion(self, both, z, i, which, energy):
        need = [q for q, p in enumerate(PAIRS) if p[0] in which or p[1] in which]
        consts = {q + o: self.ka[q + o, z, i] for q in need for o in (0, 6)}
        lengths = [self.kl[q, z, i - W] for q in range(6)] if energy else None
        found, total, b = [], None, both[0]
        for n in self.four:
            r, e = anion_terms(b, consts, lengths if n == self.counted else None, which)
            found.append(r)
            total = e if e is not None else total
            if n + 1 < self.count:
                b = self.onward((b, both[1]))
        return found, total

    def keep_forces(self, k, i, found):
        for n, f in enumerate(found):
            for j in f:
                for m in range(3):
                    self.fs[12 * n + 3 * j + m, k, i - self.ia + 1] = f[j][m]

    def owned(self, i):
        return W <= i < W + 4

    def tally(self, totals, scale, inside=None):
        totals = [t for t in totals if t is not None]
        if totals:
            total = scale * sum(totals[1:], totals[0])
            self.acc[self.e_row] += total if inside is None else jnp.where(inside, total, 0.0)

    def cation_plane(self, z, k, inside, bonds_at_start, kept):
        own = inside is not False
        totals = []
        if bonds_at_start:
            self.keep(k, self.ia - 1, self.here(z, self.ia - 1, bonds_at_start), bonds_at_start)
        for i in range(self.ia, self.ib + 1):
            both, f, e = self.cation(z, i, range(4), own and self.owned(i))
            self.keep(k, i, both, kept)
            self.keep_forces(k, i, f)
            totals.append(e)
        both, f, _ = self.cation(z, self.ib + 1, (2,), False)
        if 2 in kept:
            self.keep(k, self.ib + 1, both, (2,))
        self.keep_forces(k, self.ib + 1, f)
        self.tally(totals, 1.0, None if inside is True else inside)

    def bond_plane(self, z, k):
        for i in range(self.ia - 1, self.ib + 2):
            which = ((0, 1) if i <= self.ib else ()) + ((2,) if i >= self.ia else ())
            self.keep(k, i, self.here(z, i, which), which)

    def anion_plane(self, z, k, inside, take):
        own = inside is not False
        totals = []
        r, _ = self.anion(self.kept(k, self.ia - 1), z, self.ia - 1, (2,), False)
        before = [q[2] for q in r]
        for i in range(self.ia, self.ib + 1):
            r, e = self.anion(self.kept(k, i), z, i, range(4), own and self.owned(i))
            for n in self.four:
                for m in range(3):
                    q = [r[n][j][m] for j in range(4)]
                    take(n, m, i, q[0] + x_before(q[1]) + before[n][m], (q[0] + q[1]) + (q[2] + q[3]), q[3])
            before = [q[2] for q in r]
            totals.append(e)
        self.tally(totals, 0.5, None if inside is True else inside)

    def forces(self, k, i, n, m):
        c = i - self.ia + 1
        f = [self.fs[12 * n + 3 * j + m, k, c] for j in range(4)]
        return (f[0] + f[1]) + (f[2] + f[3]), f[0] + x_after(f[1]) + self.fs[12 * n + 6 + m, k, c + 1], f[3]

    def inner(self, za, zb, unroll):
        rs, ia, ib = self.rs, self.ia, self.ib
        count = zb - za + 1
        every = (0, 1, 2, 3)

        def cations(q):
            self.cation_plane(za + q, 1 + q, True, (0, 1, 3), every)

        loop(count, cations, unroll)
        self.cation_plane(zb + 1, count + 1, True, (0, 1, 3), every)
        self.bond_plane(za - 1, 0)

        def below(n, m, i, to_cation, to_anion, last):
            c = i - ia
            rs[3 * n + m, 0, c + 1] = last
            self.low[n, m, c] = to_cation
            self.low[n, 3 + m, c] = to_anion

        self.anion_plane(za - 1, 0, True, below)

        def anions(q):
            z, k = za + q, 1 + q

            def take(n, m, i, to_cation, to_anion, last):
                own, ahead, _ = self.forces(k, i, n, m)
                c = i - ia + 1
                rs[3 * n + m, k, c] = last
                self.emit(n, m, z, i, own + to_cation + rs[3 * n + m, k - 1, c])
                self.emit(n, 3 + m, z, i, ahead + self.fs[12 * n + 9 + m, k + 1, c] + to_anion)

            self.anion_plane(z, k, True, take)

        for q in range(count):
            anions(q)
        for i in range(ia, ib + 1):
            c = i - ia
            for n in self.four:
                for m in range(3):
                    self.low[n, 6 + m, c] = self.fs[12 * n + 9 + m, 1, c + 1]
                    own, ahead, _ = self.forces(count + 1, i, n, m)
                    self.high[n, m, c] = own
                    self.high[n, 3 + m, c] = ahead
                    self.high[n, 6 + m, c] = rs[3 * n + m, count, c + 1]
        self.keep_high(count + 1)

    def keep_high(self, k):
        for c in range(self.ib - self.ia + 3):
            for j in range(9):
                self.high[self.count, j, c] = self.bs[j, k, c]
                if self.step is not None:
                    self.high[self.count + 1, j, c] = self.ds[j, k, c]

    def lower(self, z):
        rs, ia, ib = self.rs, self.ia, self.ib
        self.cation_plane(z, 1, own_plane(z), (3,), (3,))
        self.bond_plane(z - 1, 0)

        def take(n, m, i, to_cation, to_anion, last):
            c = i - ia
            own, ahead, third = self.forces(1, i, n, m)
            self.emit(n, m, z, i, own + self.low[n, m, c] + last)
            self.emit(n, 3 + m, z, i, ahead + self.low[n, 6 + m, c] + self.low[n, 3 + m, c])
            self.low[n, m, c] = to_cation
            self.low[n, 3 + m, c] = to_anion
            self.low[n, 6 + m, c] = third

        self.anion_plane(z - 1, 0, own_plane(z - 1), take)

    def upper(self, z):
        ia, ib = self.ia, self.ib
        for c in range(ib - ia + 3):
            for j in range(9):
                self.bs[j, 2, c] = self.high[self.count, j, c]
                if self.step is not None:
                    self.ds[j, 2, c] = self.high[self.count + 1, j, c]
        self.cation_plane(z + 1, 3, own_plane(z + 1), (0, 1, 3), (0, 1, 2, 3))

        def take(n, m, i, to_cation, to_anion, last):
            c = i - ia
            own, ahead, third = self.forces(3, i, n, m)
            self.emit(n, m, z, i, self.high[n, m, c] + to_cation + self.high[n, 6 + m, c])
            self.emit(n, 3 + m, z, i, self.high[n, 3 + m, c] + third + to_anion)
            self.high[n, m, c] = own
            self.high[n, 3 + m, c] = ahead
            self.high[n, 6 + m, c] = last

        self.anion_plane(z, 2, own_plane(z), take)
        self.keep_high(3)


def own_plane(z):
    return W <= z < W + CZ


def kinds(steps, state, scratch):
    field, g0, pos1, g1, pos2, step, gs, kc, ka, kl, acc, *ends = state
    bs, fs, rs, ds = scratch[:4]
    s0, s1 = steps[0], steps[1]
    consts = (kc, ka, kl)

    def emit0(n, m, z, i, v):
        g0[m, z, i] = v
        pos1[m, z, i] = field[m, z, i] + s0 * v if m < 3 else field[m, z, i] - s0 * v

    def emit1(n, m, z, i, v):
        g1[m, z - 2, i - 2] = v
        w, d = s1 * g0[m, z, i], s1 * v
        pos2[m, z - 2, i - 2] = (pos1[m, z, i] + d) - w if m < 3 else (pos1[m, z, i] - d) + w
        step[m, z - 2, i - 2] = w if m < 3 else -w

    def emit2(n, m, z, i, v):
        gs[n, m, z - W, i - W] = v

    def at(ref):
        return lambda m, z, i: ref[m, z - 2, i - 2]

    work = (bs, ds, fs, rs)
    return (
        Kind(lambda m, z, i: field[m, z, i], None, emit0, (1, IE - 2), E0, work, consts, acc, *ends[0:2]),
        Kind(lambda m, z, i: pos1[m, z, i], None, emit1, (2, IE - 3), E1, work, consts, acc, *ends[2:4]),
        Kind(at(pos2), at(step), emit2, (W, IE - W - 1), ES + 1, work, consts, acc, *ends[4:6]),
    )


def products(state, planes):
    g0, g1, gs, acc = state[1], state[3], state[6], state[10]
    part = [None] * SUMS

    def add(n, v):
        part[n] = v if part[n] is None else part[n] + v

    for z in planes:
        for i in range(W, W + 4):
            for ch in range(6):
                a, b = g0[ch, z, i], g1[ch, z - 2, i - 2]
                g = [gs[k, ch, z - W, i - W] for k in range(4)]
                add(N0, a * a)
                add(N1, b * b)
                add(X1, a * b)
                for k in range(4):
                    add(GG1 + k, g[k] * b)
                    add(GG0 + k, g[k] * a)
                for n, (k, l) in enumerate(GPAIRS):
                    add(GG + n, g[k] * g[l])
    for n, v in enumerate(part):
        if v is not None:
            acc[n] += v


def stage_inner(own0, own1, ylo, yhi, steps, *refs):
    state, scratch = refs[:STATE], refs[STATE:]
    field, kc, ka, kl, acc = state[0], *state[7:11]
    own = (own0, own1)
    acc[...] = jnp.zeros_like(acc)

    def fill(z):
        def natural(ch, h, at):
            return own[h][pl.ds((ch * CZ + z) * CY, CY), :]

        fill_plane(field, scratch[4:6], W + z, natural, lambda r, at: y_halo(ylo, yhi, r, z, at))

    loop(CZ, fill)
    loop(CZ, lambda z: cation_constants(field, kc, W + z))
    loop(CZ - 1, lambda z: anion_constants(field, ka, kl, W + z))
    top = W + CZ - 1
    first, second, third = kinds(steps, state, scratch)
    first.inner(W + 1, top - 1, 2)
    second.inner(W + 2, top - 2, 2)
    third.inner(W + 3, top - 3, 1)
    products(state, (W + 3, top - 3))


def stage_outer(level, below, above, steps, *refs):
    state, rest = refs[STATE : 2 * STATE], refs[2 * STATE :]
    scratch = rest[1:] if level == W else rest
    field, kc, ka, kl, acc = state[0], *state[7:11]
    lo, hi = W - level, W + CZ - 1 + level
    fill_block(field, scratch[4:6], below, 0, lo)
    fill_block(field, scratch[4:6], above, 0, hi)
    if level < W:
        cation_constants(field, kc, lo)
    cation_constants(field, kc, hi)
    for z in (lo, hi - 1):
        anion_constants(field, ka, kl, z)
    for n, kind in enumerate(kinds(steps, state, scratch)):
        kind.lower(lo + 1 + n)
        kind.upper(hi - 1 - n)
    products(state, (lo + W, hi - W))
    if level < W:
        return
    sums = rest[0]
    partial = jnp.sum(acc[...], axis=1)
    row = lax.broadcasted_iota(jnp.int32, (SUMS, 128), 0)
    lane = lax.broadcasted_iota(jnp.int32, (SUMS, 128), 1)
    spread = jnp.where(row == lane, jnp.sum(partial, axis=1, keepdims=True), 0.0)
    sums[...] = jnp.broadcast_to(jnp.sum(spread, axis=0, keepdims=True), sums.shape)


def finish(cell_count, gathered, steps, g0, pos1, g1, gs, out, energies, rows0, rows1):
    total = jnp.sum(gathered[...], axis=0, keepdims=True)

    def pick(n):
        return total[:, n : n + 1]

    t = (pick(N1) - pick(X1)) / (pick(N0) + 1e-06)
    lag = (
        -t * (t - 1.0) * (t - 2.0) * (1.0 / 6.0),
        (t + 1.0) * (t - 1.0) * (t - 2.0) * 0.5,
        -(t + 1.0) * t * (t - 2.0) * 0.5,
        (t + 1.0) * t * (t - 1.0) * (1.0 / 6.0),
    )
    t2, t3, t4 = t * t, t * t * t, t * t * t * t
    area = (
        -(t4 * 0.25 - t3 + t2) * (1.0 / 6.0),
        (t4 * 0.25 - t3 * (2.0 / 3.0) - t2 * 0.5 + 2.0 * t) * 0.5,
        -(t4 * 0.25 - t3 * (1.0 / 3.0) - t2) * 0.5,
        (t4 * 0.25 - t2 * 0.5) * (1.0 / 6.0),
    )
    norm2 = sum((1.0 if k == l else 2.0) * lag[k] * lag[l] * pick(GG + n) for n, (k, l) in enumerate(GPAIRS))
    cross2 = sum(lag[k] * pick(GG1 + k) for k in range(4))
    ratio = (norm2 - cross2) / (pick(N1) + 1e-06)
    s1, s2 = steps[1], steps[2]
    energy2 = pick(ES + 1) - s1 * sum(area[k] * pick(GG0 + k) for k in range(4))
    scale = 1.0 / cell_count
    energies[0] = jnp.sum(pick(E0)) * scale
    energies[1] = jnp.sum(pick(E1)) * scale
    energies[2] = jnp.sum(energy2) * scale
    along = s1 + s2 * ratio
    weights = [jnp.broadcast_to(w, (8, 128)) for w in [s2 * q for q in lag] + [along * t, along]]

    def plane(z):
        for ch in range(6):
            for i in range(4):
                parts = [gs[k, ch, z, i] for k in range(4)]
                parts += [g0[ch, z + W, i + W], g1[ch, z + 1, i + 1]]
                v = pos1[ch, z + W, i + W]
                for weight, part in zip(weights, parts):
                    v = v + weight * part if ch < 3 else v - weight * part
                if ch >= 3:
                    v = v - H
                rows0[pl.ds(ch * CY + i, 4, stride=4), :] = v[0:4]
                rows1[pl.ds(ch * CY + i, 4, stride=4), :] = v[4:8]
        for ch in range(6):
            for h, at in halves():
                rows = (rows0, rows1)[h]
                out[pl.ds(ch * CZ * CY + z * CY, CY), at] = rows[ch * CY : (ch + 1) * CY, :]

    loop(CZ, plane)


def vmem():
    return pl.BlockSpec(memory_space=pltpu.VMEM)


def smem():
    return pl.BlockSpec(memory_space=pltpu.SMEM)


def params(mib):
    return pltpu.CompilerParams(vmem_limit_bytes=mib * MIB)


def ring(value, axis, step):
    n = lax.axis_size(axis)
    return lax.ppermute(value, axis, [(i, (i + step) % n) for i in range(n)])


def per_device(displacement, species, step_sizes):
    shape = jax.ShapeDtypeStruct
    devices = lax.axis_size("slab") * lax.axis_size("col")
    cell_count = devices * CZ * CY * NX
    disp = displacement.reshape(6 * CZ * CY, NX)
    spec = species.reshape(CZ * CY, NX)
    edge = shape((W * CZ * 8, NX), f32)
    blocks = tuple(shape((len(planes) * PLANE, NX), f32) for planes in BLOCKS)
    half = shape((8 * CZ * CY, 128), f32)
    yup, ydown, *packed = pl.pallas_call(
        pack,
        out_shape=(edge, edge, *blocks, half, half),
        in_specs=[pl.BlockSpec(memory_space=pltpu.HBM)] * 2,
        out_specs=[vmem()] * (4 + len(blocks)),
        scratch_shapes=[
            pltpu.VMEM((6 * CZ * CY, NX), f32),
            pltpu.VMEM((CZ * CY, NX), jnp.int32),
            pltpu.SemaphoreType.DMA((2,)),
        ],
        compiler_params=params(4),
        name="pack",
    )(disp, spec)
    own = packed[-2:]
    ylo, yhi = ring(yup, "col", 1), ring(ydown, "col", -1)
    ups = pl.pallas_call(
        pack_halo,
        out_shape=blocks,
        in_specs=[vmem()] * (2 + len(blocks)),
        out_specs=[vmem()] * len(blocks),
        input_output_aliases={2 + n: n for n in range(len(blocks))},
        compiler_params=params(4),
        name="pack_halo",
    )(ylo, yhi, *packed[: len(blocks)])

    def travel(level):
        return ring(ups[2 * level], "slab", 1), ring(ups[2 * level + 1], "slab", -1)

    def tiles(*lead):
        return (*lead, 8, 128)

    state_shapes = tuple(
        shape(tiles(*lead), f32)
        for lead in (
            (7, ZE, IE),
            (6, ZE, IE),
            (6, ZE, IE),
            (6, ZE - 4, IE - 4),
            (6, ZE - 4, IE - 4),
            (6, ZE - 4, IE - 4),
            (4, 6, CZ, 4),
            (6, ZE, IE),
            (12, ZE - 1, IE - 1),
            (6, ZE, 4),
            (SUMS,),
            (1, 9, 8),
            (2, 9, 10),
            (1, 9, 6),
            (2, 9, 8),
            (4, 9, 4),
            (6, 9, 6),
        )
    )
    scratch = [
        pltpu.VMEM(tiles(12 * CZ * IE), f32),
        pltpu.VMEM(tiles(48 * 4 * 6), f32),
        pltpu.VMEM(tiles(3 * CZ * IE + 48), f32),
        pltpu.VMEM(tiles(12 * 4 * 6), f32),
        pltpu.VMEM((8 * 32, 128), f32),
        pltpu.VMEM((8 * 32, 128), f32),
    ]
    near = [travel(0), travel(1)]
    state = pl.pallas_call(
        stage_inner,
        out_shape=state_shapes,
        in_specs=[vmem()] * 4 + [smem()],
        out_specs=[vmem()] * STATE,
        scratch_shapes=scratch,
        compiler_params=params(17),
        cost_estimate=pl.CostEstimate(flops=100000000, bytes_accessed=1000000, transcendentals=0),
        name="stage_inner",
    )(*own, ylo, yhi, step_sizes)
    state = list(state)
    *last, state[10] = lax.optimization_barrier((*ups[4:6], state[10]))
    ups = (*ups[:4], *last)
    arrivals = near + [travel(2)]
    for level in range(1, W + 1):
        final = level == W
        *state, = pl.pallas_call(
            functools.partial(stage_outer, level),
            out_shape=(*state_shapes, shape((devices, 128), f32)) if final else state_shapes,
            in_specs=[vmem()] * 2 + [smem()] + [vmem()] * STATE,
            out_specs=[vmem()] * (STATE + final),
            scratch_shapes=scratch,
            input_output_aliases={3 + n: n for n in range(STATE)},
            compiler_params=params(17),
            cost_estimate=pl.CostEstimate(flops=100000000, bytes_accessed=1000000, transcendentals=0),
            name="stage_outer",
        )(*arrivals[level - 1], step_sizes, *state)
    sums = state.pop()
    gathered = lax.all_to_all(sums.reshape(devices, 1, 128), ("slab", "col"), 0, 0)
    relaxed, energies = pl.pallas_call(
        functools.partial(finish, cell_count),
        out_shape=(shape((6 * CZ * CY, NX), f32), shape((3,), f32)),
        in_specs=[vmem(), smem()] + [vmem()] * 4,
        out_specs=[vmem(), smem()],
        scratch_shapes=[pltpu.VMEM((6 * CY, 128), f32)] * 2,
        compiler_params=params(4),
        name="finish",
    )(gathered.reshape(devices, 128), step_sizes, *state[1:4], state[6])
    return relaxed.reshape(displacement.shape), energies


def solution(mesh):
    in_specs = (P(None, "slab", "col", None), P("slab", "col", None), P())
    out_specs = (P(None, "slab", "col", None), P())
    return jax.shard_map(
        per_device, mesh=mesh, in_specs=in_specs, out_specs=out_specs, check_vma=False
    )
```

```python
import functools

import jax
import jax.numpy as jnp
from jax import lax
from jax.experimental import pallas as pl
from jax.experimental.pallas import tpu as pltpu
from jax.sharding import PartitionSpec as P

CZ, CY, NX = 8, 16, 256
W = 3
ZE = CZ + 2 * W
IE = 4 + 2 * W
ROWS = (-3, -2, -1, 16, 17, 18)
PLANE = 7 * CY
H = 4.0 / 3.0**0.5
SIGNS = ((1, 1, 1), (1, -1, -1), (-1, 1, -1), (-1, -1, 1))
PAIRS = ((0, 1), (0, 2), (0, 3), (1, 2), (1, 3), (2, 3))
SAMPLES = (-1.0, 0.0, 1.0, 2.0)
E0, E1, ES, N0, N1, X1, GG1, GG0, GG = 0, 1, 2, 6, 7, 8, 9, 13, 17
GPAIRS = tuple((k, l) for k in range(4) for l in range(k, 4))
SUMS = 32
UP = ((7, (1, 2, 3, 4, 5)), (6, (2, 3, 4, 5)), (5, (3, 4, 5)))
DOWN = ((0, (0, 1, 2, 3, 4)), (1, (0, 1, 2, 3)), (2, (0, 1, 2)))
BLOCKS = (UP[:2], DOWN[:2], UP[2:], DOWN[2:])
MIB = 1024 * 1024
STATE = 17
f32 = jnp.float32


def halves():
    return (0, slice(0, 128)), (1, slice(128, NX))


def block_rows(block):
    return len(block) * PLANE + 8 * sum(len(rows) for _, rows in block)


def halo_at(block):
    at = len(block) * PLANE
    for k, (z, rows) in enumerate(block):
        for r in rows:
            yield at, k, z, r
            at += 8


def pack(given, yup, ydown, *refs):
    blocks, own, steps = refs[: len(BLOCKS)], refs[len(BLOCKS) : len(BLOCKS) + 2], refs[-1]
    for n in range(3):
        steps[n] = jnp.broadcast_to(given[7 * CZ * CY + n : 7 * CZ * CY + n + 1, 0:128], (8, 128))
    for h, at in halves():
        rows = own[h]
        rows[0 : 7 * CZ * CY, :] = given[0 : 7 * CZ * CY, at]
        rows[7 * CZ * CY :, :] = jnp.zeros((CZ * CY, 128), f32)
        for dst, first in ((yup, CY - W), (ydown, 0)):
            for r in range(W):
                for z in range(CZ):
                    to = (r * CZ + z) * 8
                    dst[to : to + 8, at] = rows[pl.ds(z * CY + first + r, 8, stride=CZ * CY), :]
    for dst, block in zip(blocks, BLOCKS):
        for k, (z, _) in enumerate(block):
            for ch in range(7):
                to, first = k * PLANE + ch * CY, (ch * CZ + z) * CY
                dst[to : to + CY, :] = given[first : first + CY, :]


def y_halo(ylo, yhi, r, z, at=slice(None)):
    src = ylo if r < W else yhi
    return src[pl.ds((r % W) * CZ * 8 + z * 8, 8), at]


def pack_halo(ylo, yhi, *refs):
    for dst, block in zip(refs[len(BLOCKS) :], BLOCKS):
        for at, _, z, r in halo_at(block):
            dst[at : at + 8, :] = y_halo(ylo, yhi, r, z)


def lanes():
    return lax.broadcasted_iota(jnp.int32, (8, 128), 1)


def x_before(v):
    r = pltpu.roll(v, 1, 1)
    return jnp.where(lanes() == 0, pltpu.roll(r, 4, 0), r)


def x_after(v):
    r = pltpu.roll(v, 127, 1)
    return jnp.where(lanes() == 127, pltpu.roll(r, 4, 0), r)


def dot(a, b):
    return a[0] * b[0] + a[1] * b[1] + a[2] * b[2]


def loop(n, body, unroll=1):
    def step(k, carry):
        for q in range(unroll):
            body(k * unroll + q)
        return carry

    full = n // unroll
    if full > 1:
        lax.fori_loop(0, full, step, 0)
    else:
        full = 0
    for q in range(full * unroll, n):
        body(q)


def fill_plane(field, both, z, natural, halo):
    for h, at in halves():
        rows = both[h]
        for ch in range(7):
            rows[ch * 32 + 8 : ch * 32 + 24, :] = natural(ch, h, at)
        for r, y in enumerate(ROWS):
            if halo(r, at) is not None:
                rows[pl.ds(y + 8, 8, stride=32), :] = halo(r, at)
        for ch in range(7):
            for i in range(IE):
                first = ch * 32 + 8 - W + i
                v = rows[pl.ds(first, 4, stride=4), :]
                field[ch, z, i, 4 * h : 4 * h + 4, :] = v + H if 3 <= ch < 6 else v


def fill_block(field, both, src, block, k, z):
    places = {r: at for at, n, _, r in halo_at(block) if n == k}
    fill_plane(
        field,
        both,
        z,
        lambda ch, h, at: src[pl.ds(k * PLANE + ch * CY, CY), at],
        lambda r, at: src[pl.ds(places[r], 8), at] if r in places else None,
    )


def cation_constants(field, kc, z):
    for i in range(1, IE):
        indium = field[6, z, i] < 0.5

        def pick(fn):
            return jnp.where(indium, fn(0.848, 0.132, 4.28), fn(1.0, 0.215, 4.0)).astype(f32)

        kc[0, z, i] = pick(lambda a, b, l: 0.75 * a / l**2)
        kc[1, z, i] = pick(lambda a, b, l: -0.75 * a)
        kc[2, z, i] = pick(lambda a, b, l: 0.75 * b / l**2)
        kc[3, z, i] = pick(lambda a, b, l: 0.25 * b)
        kc[4, z, i] = pick(lambda a, b, l: l**2 / (3.0 * a))
        kc[5, z, i] = pick(lambda a, b, l: l**2 / (1.5 * b))


def anion_constants(field, ka, kl, z):
    for i in range(0, IE - 1):
        s = (field[6, z, i], x_after(field[6, z, i]), field[6, z, i + 1], field[6, z + 1, i])
        for q, (j, l) in enumerate(PAIRS):
            t = s[j] + s[l]

            def pick(fn):
                ii = fn(0.264, 4.28 * 4.28)
                mixed = fn(0.347, 4.28 * 4.0)
                gg = fn(0.43, 16.0)
                return jnp.where(t < 0.5, ii, jnp.where(t < 1.5, mixed, gg)).astype(f32)

            ka[q, z, i] = pick(lambda b, ll: 0.375 * b / ll)
            ka[6 + q, z, i] = pick(lambda b, ll: 0.125 * b)
            if W <= i < W + 4:
                kl[q, z, i - W] = pick(lambda b, ll: ll / 3.0)


OFFSETS = ((0, 0), (0, 0), (0, 1), (1, 0))


class Tiles:
    def __init__(self, ref, planes, cells):
        self.ref, self.planes, self.cells = ref, planes, cells

    def at(self, key):
        n, k, i = key
        return (n * self.planes + k) * self.cells + i

    def __getitem__(self, key):
        return self.ref[self.at(key)]

    def __setitem__(self, key, value):
        self.ref[self.at(key)] = value


def bonds(pos, z, i, which, h):
    found = {}
    cat = [pos(m, z, i) for m in range(3)]
    lo, hi = cat, (cat if h == 0 else [c + 2.0 * h for c in cat])
    for j in which:
        dz, di = OFFSETS[j]
        b = []
        for m in range(3):
            a = pos(3 + m, z - dz, i - di)
            if j == 1:
                a = x_before(a)
            b.append(a - (lo[m] if SIGNS[j][m] > 0 else hi[m]))
        found[j] = b
    return found


def cation_terms(b, k, which, energy):
    e = {}
    for j in range(4):
        for l in range(j, 4):
            if j not in which and l not in which:
                continue
            d = dot(b[j], b[l])
            e[j, l] = e[l, j] = k[0] * d + k[1] if j == l else k[2] * d + k[3]
    f = {j: [sum(e[j, l] * b[l][m] for l in range(4)) for m in range(3)] for j in which}
    total = None
    if energy:
        diag = sum(e[j, j] * e[j, j] for j in range(4))
        off = sum(e[p] * e[p] for p in PAIRS)
        total = diag * k[4] + off * k[5]
    return f, total


def anion_terms(b, k, lengths, which):
    c, total = {}, None
    for q, (j, l) in enumerate(PAIRS):
        if j not in which and l not in which:
            continue
        d = dot(b[j], b[l])
        c[j, l] = c[l, j] = k[q] * d + k[6 + q]
        if lengths is not None:
            part = c[j, l] * (d + lengths[q])
            total = part if total is None else total + part
    r = {j: [sum(c[j, l] * b[l][m] for l in range(4) if l != j) for m in range(3)] for j in which}
    return r, total


class Kind:
    def __init__(self, pos, step, emit, cells, e_row, scratch, consts, acc, low, high):
        self.pos, self.step, self.emit, self.e_row = pos, step, emit, e_row
        self.ia, self.ib = cells
        self.kc, self.ka, self.kl = consts
        self.acc, self.low, self.high = acc, low, high
        self.four = range(1 if step is None else 4)
        self.count = len(self.four)
        planes = CZ if step is None else 4
        width = self.ib - self.ia + 3
        self.bs, self.ds, self.fs, self.rs = (Tiles(ref, planes, width) for ref in scratch)
        self.counted = 0 if step is None else 1

    def here(self, z, i, which):
        b = bonds(self.pos, z, i, which, H)
        return b, None if self.step is None else bonds(self.step, z, i, which, 0)

    def keep(self, k, i, both, which):
        c = i - self.ia + 1
        for dst, v in zip((self.bs, self.ds), both):
            if v is not None:
                for j in which:
                    for m in range(3):
                        dst[3 * j + m, k, c] = x_after(v[j][m]) if j == 1 else v[j][m]

    def kept(self, k, i):
        c = i - self.ia + 1
        both = [self.bs, self.ds] if self.step is not None else [self.bs]
        return [{j: [src[3 * j + m, k + OFFSETS[j][0], c + OFFSETS[j][1]] for m in range(3)] for j in range(4)} for src in both]

    def onward(self, both):
        b, d = both[0], both[1] if len(both) > 1 else None
        return b if d is None else {j: [b[j][m] + d[j][m] for m in range(3)] for j in b}

    def cation(self, z, i, which, energy):
        both = self.here(z, i, range(4))
        consts = [self.kc[n, z, i] for n in range(6 if energy else 4)]
        found, total, b = [], None, both[0]
        for n in self.four:
            f, e = cation_terms(b, consts, which, energy and n == self.counted)
            found.append(f)
            total = e if e is not None else total
            if n + 1 < self.count:
                b = self.onward((b, both[1]))
        return both, found, total

    def anion(self, both, z, i, which, energy):
        need = [q for q, p in enumerate(PAIRS) if p[0] in which or p[1] in which]
        consts = {q + o: self.ka[q + o, z, i] for q in need for o in (0, 6)}
        lengths = [self.kl[q, z, i - W] for q in range(6)] if energy else None
        found, total, b = [], None, both[0]
        for n in self.four:
            r, e = anion_terms(b, consts, lengths if n == self.counted else None, which)
            found.append(r)
            total = e if e is not None else total
            if n + 1 < self.count:
                b = self.onward((b, both[1]))
        return found, total

    def keep_forces(self, k, i, found):
        for n, f in enumerate(found):
            for j in f:
                for m in range(3):
                    self.fs[12 * n + 3 * j + m, k, i - self.ia + 1] = f[j][m]

    def owned(self, i):
        return W <= i < W + 4

    def tally(self, totals, scale, inside=None):
        totals = [t for t in totals if t is not None]
        if totals:
            total = scale * sum(totals[1:], totals[0])
            self.acc[self.e_row] += total if inside is None else jnp.where(inside, total, 0.0)

    def cation_plane(self, z, k, inside, bonds_at_start, kept):
        own = inside is not False
        totals = []
        if bonds_at_start:
            self.keep(k, self.ia - 1, self.here(z, self.ia - 1, bonds_at_start), bonds_at_start)
        for i in range(self.ia, self.ib + 1):
            both, f, e = self.cation(z, i, range(4), own and self.owned(i))
            self.keep(k, i, both, kept)
            self.keep_forces(k, i, f)
            totals.append(e)
        both, f, _ = self.cation(z, self.ib + 1, (2,), False)
        if 2 in kept:
            self.keep(k, self.ib + 1, both, (2,))
        self.keep_forces(k, self.ib + 1, f)
        self.tally(totals, 1.0, None if inside is True else inside)

    def bond_plane(self, z, k):
        for i in range(self.ia - 1, self.ib + 2):
            which = ((0, 1) if i <= self.ib else ()) + ((2,) if i >= self.ia else ())
            self.keep(k, i, self.here(z, i, which), which)

    def anion_plane(self, z, k, inside, take):
        own = inside is not False
        totals = []
        r, _ = self.anion(self.kept(k, self.ia - 1), z, self.ia - 1, (2,), False)
        before = [q[2] for q in r]
        for i in range(self.ia, self.ib + 1):
            r, e = self.anion(self.kept(k, i), z, i, range(4), own and self.owned(i))
            for n in self.four:
                for m in range(3):
                    q = [r[n][j][m] for j in range(4)]
                    take(n, m, i, q[0] + x_before(q[1]) + before[n][m], (q[0] + q[1]) + (q[2] + q[3]), q[3])
            before = [q[2] for q in r]
            totals.append(e)
        self.tally(totals, 0.5, None if inside is True else inside)

    def forces(self, k, i, n, m):
        c = i - self.ia + 1
        f = [self.fs[12 * n + 3 * j + m, k, c] for j in range(4)]
        return (f[0] + f[1]) + (f[2] + f[3]), f[0] + x_after(f[1]) + self.fs[12 * n + 6 + m, k, c + 1], f[3]

    def inner(self, za, zb, unroll):
        rs, ia, ib = self.rs, self.ia, self.ib
        count = zb - za + 1
        every = (0, 1, 2, 3)

        def cations(q):
            self.cation_plane(za + q, 1 + q, True, (0, 1, 3), every)

        loop(count, cations, unroll)
        self.cation_plane(zb + 1, count + 1, True, (0, 1, 3), every)
        self.bond_plane(za - 1, 0)

        def below(n, m, i, to_cation, to_anion, last):
            c = i - ia
            rs[3 * n + m, 0, c + 1] = last
            self.low[n, m, c] = to_cation
            self.low[n, 3 + m, c] = to_anion

        self.anion_plane(za - 1, 0, True, below)

        def anions(q):
            z, k = za + q, 1 + q

            def take(n, m, i, to_cation, to_anion, last):
                own, ahead, _ = self.forces(k, i, n, m)
                c = i - ia + 1
                rs[3 * n + m, k, c] = last
                self.emit(n, m, z, i, own + to_cation + rs[3 * n + m, k - 1, c])
                self.emit(n, 3 + m, z, i, ahead + self.fs[12 * n + 9 + m, k + 1, c] + to_anion)

            self.anion_plane(z, k, True, take)

        for q in range(count):
            anions(q)
        for i in range(ia, ib + 1):
            c = i - ia
            for n in self.four:
                for m in range(3):
                    self.low[n, 6 + m, c] = self.fs[12 * n + 9 + m, 1, c + 1]
                    own, ahead, _ = self.forces(count + 1, i, n, m)
                    self.high[n, m, c] = own
                    self.high[n, 3 + m, c] = ahead
                    self.high[n, 6 + m, c] = rs[3 * n + m, count, c + 1]
        self.keep_high(count + 1)

    def keep_high(self, k):
        for c in range(self.ib - self.ia + 3):
            for j in range(9):
                self.high[self.count, j, c] = self.bs[j, k, c]
                if self.step is not None:
                    self.high[self.count + 1, j, c] = self.ds[j, k, c]

    def lower(self, z):
        rs, ia, ib = self.rs, self.ia, self.ib
        self.cation_plane(z, 1, own_plane(z), (3,), (3,))
        self.bond_plane(z - 1, 0)

        def take(n, m, i, to_cation, to_anion, last):
            c = i - ia
            own, ahead, third = self.forces(1, i, n, m)
            self.emit(n, m, z, i, own + self.low[n, m, c] + last)
            self.emit(n, 3 + m, z, i, ahead + self.low[n, 6 + m, c] + self.low[n, 3 + m, c])
            self.low[n, m, c] = to_cation
            self.low[n, 3 + m, c] = to_anion
            self.low[n, 6 + m, c] = third

        self.anion_plane(z - 1, 0, own_plane(z - 1), take)

    def upper(self, z):
        ia, ib = self.ia, self.ib
        for c in range(ib - ia + 3):
            for j in range(9):
                self.bs[j, 2, c] = self.high[self.count, j, c]
                if self.step is not None:
                    self.ds[j, 2, c] = self.high[self.count + 1, j, c]
        self.cation_plane(z + 1, 3, own_plane(z + 1), (0, 1, 3), (0, 1, 2, 3))

        def take(n, m, i, to_cation, to_anion, last):
            c = i - ia
            own, ahead, third = self.forces(3, i, n, m)
            self.emit(n, m, z, i, self.high[n, m, c] + to_cation + self.high[n, 6 + m, c])
            self.emit(n, 3 + m, z, i, self.high[n, 3 + m, c] + third + to_anion)
            self.high[n, m, c] = own
            self.high[n, 3 + m, c] = ahead
            self.high[n, 6 + m, c] = last

        self.anion_plane(z, 2, own_plane(z), take)
        self.keep_high(3)


def own_plane(z):
    return W <= z < W + CZ


def kinds(steps, state, scratch):
    field, g0, pos1, g1, pos2, step, gs, kc, ka, kl, acc, *ends = state
    bs, fs, rs, ds = scratch[:4]
    s0, s1 = steps[0], steps[1]
    consts = (kc, ka, kl)

    def emit0(n, m, z, i, v):
        g0[m, z, i] = v
        pos1[m, z, i] = field[m, z, i] + s0 * v if m < 3 else field[m, z, i] - s0 * v

    def emit1(n, m, z, i, v):
        g1[m, z - 2, i - 2] = v
        w, d = s1 * g0[m, z, i], s1 * v
        pos2[m, z - 2, i - 2] = (pos1[m, z, i] + d) - w if m < 3 else (pos1[m, z, i] - d) + w
        step[m, z - 2, i - 2] = w if m < 3 else -w

    def emit2(n, m, z, i, v):
        gs[n, m, z - W, i - W] = v

    def at(ref):
        return lambda m, z, i: ref[m, z - 2, i - 2]

    work = (bs, ds, fs, rs)
    return (
        Kind(lambda m, z, i: field[m, z, i], None, emit0, (1, IE - 2), E0, work, consts, acc, *ends[0:2]),
        Kind(lambda m, z, i: pos1[m, z, i], None, emit1, (2, IE - 3), E1, work, consts, acc, *ends[2:4]),
        Kind(at(pos2), at(step), emit2, (W, IE - W - 1), ES + 1, work, consts, acc, *ends[4:6]),
    )


def products(state, planes):
    g0, g1, gs, acc = state[1], state[3], state[6], state[10]
    part = [None] * SUMS

    def add(n, v):
        part[n] = v if part[n] is None else part[n] + v

    for z in planes:
        for i in range(W, W + 4):
            for ch in range(6):
                a, b = g0[ch, z, i], g1[ch, z - 2, i - 2]
                g = [gs[k, ch, z - W, i - W] for k in range(4)]
                add(N0, a * a)
                add(N1, b * b)
                add(X1, a * b)
                for k in range(4):
                    add(GG1 + k, g[k] * b)
                    add(GG0 + k, g[k] * a)
                for n, (k, l) in enumerate(GPAIRS):
                    add(GG + n, g[k] * g[l])
    for n, v in enumerate(part):
        if v is not None:
            acc[n] += v


def stage_inner(own0, own1, ylo, yhi, steps, *refs):
    state, scratch = refs[:STATE], refs[STATE:]
    field, kc, ka, kl, acc = state[0], *state[7:11]
    own = (own0, own1)
    acc[...] = jnp.zeros_like(acc)

    def fill(z):
        def natural(ch, h, at):
            return own[h][pl.ds((ch * CZ + z) * CY, CY), :]

        fill_plane(field, scratch[4:6], W + z, natural, lambda r, at: y_halo(ylo, yhi, r, z, at))

    loop(CZ, fill)
    loop(CZ, lambda z: cation_constants(field, kc, W + z))
    loop(CZ - 1, lambda z: anion_constants(field, ka, kl, W + z))
    top = W + CZ - 1
    first, second, third = kinds(steps, state, scratch)
    first.inner(W + 1, top - 1, 2)
    second.inner(W + 2, top - 2, 2)
    third.inner(W + 3, top - 3, 1)
    products(state, (W + 3, top - 3))


def stage_outer(levels, below, above, steps, *refs):
    state, rest = refs[STATE : 2 * STATE], refs[2 * STATE :]
    final = levels[-1] == W
    scratch = rest[1:] if final else rest
    field, kc, ka, kl, acc = state[0], *state[7:11]
    for k, level in enumerate(levels):
        lo, hi = W - level, W + CZ - 1 + level
        fill_block(field, scratch[4:6], below, UP[levels[0] - 1 : levels[-1]], k, lo)
        fill_block(field, scratch[4:6], above, DOWN[levels[0] - 1 : levels[-1]], k, hi)
        if level < W:
            cation_constants(field, kc, lo)
        cation_constants(field, kc, hi)
        for z in (lo, hi - 1):
            anion_constants(field, ka, kl, z)
        for n, kind in enumerate(kinds(steps, state, scratch)):
            kind.lower(lo + 1 + n)
            kind.upper(hi - 1 - n)
        products(state, (lo + W, hi - W))
    if not final:
        return
    sums = rest[0]
    partial = jnp.sum(acc[...], axis=1)
    row = lax.broadcasted_iota(jnp.int32, (SUMS, 128), 0)
    lane = lax.broadcasted_iota(jnp.int32, (SUMS, 128), 1)
    spread = jnp.where(row == lane, jnp.sum(partial, axis=1, keepdims=True), 0.0)
    sums[...] = jnp.broadcast_to(jnp.sum(spread, axis=0, keepdims=True), sums.shape)


def finish(cell_count, gathered, steps, g0, pos1, g1, gs, out_hbm, energies, rows0, rows1, out, sems):
    total = jnp.sum(gathered[...], axis=0, keepdims=True)

    def pick(n):
        return total[:, n : n + 1]

    t = (pick(N1) - pick(X1)) / (pick(N0) + 1e-06)
    lag = (
        -t * (t - 1.0) * (t - 2.0) * (1.0 / 6.0),
        (t + 1.0) * (t - 1.0) * (t - 2.0) * 0.5,
        -(t + 1.0) * t * (t - 2.0) * 0.5,
        (t + 1.0) * t * (t - 1.0) * (1.0 / 6.0),
    )
    t2, t3, t4 = t * t, t * t * t, t * t * t * t
    area = (
        -(t4 * 0.25 - t3 + t2) * (1.0 / 6.0),
        (t4 * 0.25 - t3 * (2.0 / 3.0) - t2 * 0.5 + 2.0 * t) * 0.5,
        -(t4 * 0.25 - t3 * (1.0 / 3.0) - t2) * 0.5,
        (t4 * 0.25 - t2 * 0.5) * (1.0 / 6.0),
    )
    norm2 = sum((1.0 if k == l else 2.0) * lag[k] * lag[l] * pick(GG + n) for n, (k, l) in enumerate(GPAIRS))
    cross2 = sum(lag[k] * pick(GG1 + k) for k in range(4))
    ratio = (norm2 - cross2) / (pick(N1) + 1e-06)
    s1, s2 = steps[1][0:1, 0:1], steps[2][0:1, 0:1]
    energy2 = pick(ES + 1) - s1 * sum(area[k] * pick(GG0 + k) for k in range(4))
    scale = 1.0 / cell_count
    energies[0] = jnp.sum(pick(E0)) * scale
    energies[1] = jnp.sum(pick(E1)) * scale
    energies[2] = jnp.sum(energy2) * scale
    along = s1 + s2 * ratio
    weights = [jnp.broadcast_to(w, (8, 128)) for w in [s2 * q for q in lag] + [along * t, along]]

    copies = []
    for ch in range(6):

        def plane(z):
            for i in range(4):
                parts = [gs[k, ch, z, i] for k in range(4)]
                parts += [g0[ch, z + W, i + W], g1[ch, z + 1, i + 1]]
                v = pos1[ch, z + W, i + W]
                for weight, part in zip(weights, parts):
                    v = v + weight * part if ch < 3 else v - weight * part
                if ch >= 3:
                    v = v - H
                rows0[pl.ds(z * CY + i, 4, stride=4), :] = v[0:4]
                rows1[pl.ds(z * CY + i, 4, stride=4), :] = v[4:8]

        loop(CZ, plane, 2)
        to = slice(ch * CZ * CY, (ch + 1) * CZ * CY)
        for h, at in halves():
            out[to, at] = (rows0, rows1)[h][...]
        copies.append(pltpu.make_async_copy(out.at[to], out_hbm.at[to], sems.at[ch]))
        copies[-1].start()
    for copy in copies:
        copy.wait()


def vmem():
    return pl.BlockSpec(memory_space=pltpu.VMEM)


def smem():
    return pl.BlockSpec(memory_space=pltpu.SMEM)


def params(mib):
    return pltpu.CompilerParams(vmem_limit_bytes=mib * MIB)


def ring(value, axis, step):
    n = lax.axis_size(axis)
    return lax.ppermute(value, axis, [(i, (i + step) % n) for i in range(n)])


def per_device(displacement, species, step_sizes):
    shape = jax.ShapeDtypeStruct
    devices = lax.axis_size("slab") * lax.axis_size("col")
    cell_count = devices * CZ * CY * NX
    spec = species.reshape(CZ * CY, NX).astype(f32)
    steps = jnp.pad(jnp.broadcast_to(step_sizes[:, None], (3, NX)), ((0, 5), (0, 0)))
    given = jnp.concatenate([displacement.reshape(6 * CZ * CY, NX), spec, steps])
    edge = shape((W * CZ * 8, NX), f32)
    blocks = tuple(shape((block_rows(block), NX), f32) for block in BLOCKS)
    half = shape((8 * CZ * CY, 128), f32)
    yup, ydown, *packed, steps = pl.pallas_call(
        pack,
        out_shape=(edge, edge, *blocks, half, half, shape((3, 8, 128), f32)),
        in_specs=[vmem()],
        out_specs=[vmem()] * (5 + len(blocks)),
        compiler_params=params(4),
        name="pack",
    )(given)
    own = packed[-2:]
    ylo, yhi = ring(yup, "col", 1), ring(ydown, "col", -1)
    ups = pl.pallas_call(
        pack_halo,
        out_shape=blocks,
        in_specs=[vmem()] * (2 + len(blocks)),
        out_specs=[vmem()] * len(blocks),
        input_output_aliases={2 + n: n for n in range(len(blocks))},
        compiler_params=params(4),
        name="pack_halo",
    )(ylo, yhi, *packed[: len(blocks)])

    def travel(level):
        return ring(ups[2 * level], "slab", 1), ring(ups[2 * level + 1], "slab", -1)

    def tiles(*lead):
        return (*lead, 8, 128)

    state_shapes = tuple(
        shape(tiles(*lead), f32)
        for lead in (
            (7, ZE, IE),
            (6, ZE, IE),
            (6, ZE, IE),
            (6, ZE - 4, IE - 4),
            (6, ZE - 4, IE - 4),
            (6, ZE - 4, IE - 4),
            (4, 6, CZ, 4),
            (6, ZE, IE),
            (12, ZE - 1, IE - 1),
            (6, ZE, 4),
            (SUMS,),
            (1, 9, 8),
            (2, 9, 10),
            (1, 9, 6),
            (2, 9, 8),
            (4, 9, 4),
            (6, 9, 6),
        )
    )
    scratch = [
        pltpu.VMEM(tiles(12 * CZ * IE), f32),
        pltpu.VMEM(tiles(48 * 4 * 6), f32),
        pltpu.VMEM(tiles(3 * CZ * IE + 48), f32),
        pltpu.VMEM(tiles(12 * 4 * 6), f32),
        pltpu.VMEM((8 * 32, 128), f32),
        pltpu.VMEM((8 * 32, 128), f32),
    ]
    near = travel(0)
    state = pl.pallas_call(
        stage_inner,
        out_shape=state_shapes,
        in_specs=[vmem()] * 5,
        out_specs=[vmem()] * STATE,
        scratch_shapes=scratch,
        compiler_params=params(17),
        cost_estimate=pl.CostEstimate(flops=100000000, bytes_accessed=1000000, transcendentals=0),
        name="stage_inner",
    )(*own, ylo, yhi, steps)
    state = list(state)
    *last, state[10] = lax.optimization_barrier((*ups[2:4], state[10]))
    ups = (*ups[:2], *last)
    for levels, arrived in (((1, 2), near), ((3,), travel(1))):
        final = levels[-1] == W
        state = pl.pallas_call(
            functools.partial(stage_outer, levels),
            out_shape=(*state_shapes, shape((devices, 128), f32)) if final else state_shapes,
            in_specs=[vmem()] * (3 + STATE),
            out_specs=[vmem()] * (STATE + final),
            scratch_shapes=scratch,
            input_output_aliases={3 + n: n for n in range(STATE)},
            compiler_params=params(17),
            cost_estimate=pl.CostEstimate(flops=100000000, bytes_accessed=1000000, transcendentals=0),
            name="stage_outer",
        )(*arrived, steps, *state)
    *state, sums = state
    gathered = lax.all_to_all(sums.reshape(devices, 1, 128), ("slab", "col"), 0, 0)
    relaxed, energies = pl.pallas_call(
        functools.partial(finish, cell_count),
        out_shape=(shape((6 * CZ * CY, NX), f32), shape((3,), f32)),
        in_specs=[vmem()] * 6,
        out_specs=[pl.BlockSpec(memory_space=pltpu.HBM), smem()],
        scratch_shapes=[
            pltpu.VMEM((CZ * CY, 128), f32),
            pltpu.VMEM((CZ * CY, 128), f32),
            pltpu.VMEM((6 * CZ * CY, NX), f32),
            pltpu.SemaphoreType.DMA((6,)),
        ],
        compiler_params=params(4),
        name="finish",
    )(gathered.reshape(devices, 128), steps, *state[1:4], state[6])
    return relaxed.reshape(displacement.shape), energies


def solution(mesh):
    in_specs = (P(None, "slab", "col", None), P("slab", "col", None), P())
    out_specs = (P(None, "slab", "col", None), P())
    return jax.shard_map(
        per_device, mesh=mesh, in_specs=in_specs, out_specs=out_specs, check_vma=False
    )
```

```python
import functools

import jax
import jax.numpy as jnp
from jax import lax
from jax.experimental import pallas as pl
from jax.experimental.pallas import tpu as pltpu
from jax.sharding import PartitionSpec as P

CZ, CY, NX = 8, 16, 256
W = 3
ZE = CZ + 2 * W
IE = 4 + 2 * W
ROWS = (-3, -2, -1, 16, 17, 18)
PLANE = 7 * CY
H = 4.0 / 3.0**0.5
SIGNS = ((1, 1, 1), (1, -1, -1), (-1, 1, -1), (-1, -1, 1))
PAIRS = ((0, 1), (0, 2), (0, 3), (1, 2), (1, 3), (2, 3))
SAMPLES = (-1.0, 0.0, 1.0, 2.0)
E0, E1, ES, N0, N1, X1, GG1, GG0, GG = 0, 1, 2, 6, 7, 8, 9, 13, 17
GPAIRS = tuple((k, l) for k in range(4) for l in range(k, 4))
SUMS = 32
UP = ((7, (1, 2, 3, 4, 5)), (6, (2, 3, 4, 5)), (5, (3, 4, 5)))
DOWN = ((0, (0, 1, 2, 3, 4)), (1, (0, 1, 2, 3)), (2, (0, 1, 2)))
BLOCKS = (UP[:2], DOWN[:2], UP[2:], DOWN[2:])
MIB = 1024 * 1024
STATE = 17
f32 = jnp.float32


def halves():
    return (0, slice(0, 128)), (1, slice(128, NX))


def block_rows(block):
    return len(block) * PLANE + 8 * sum(len(rows) for _, rows in block)


def halo_at(block):
    at = len(block) * PLANE
    for k, (z, rows) in enumerate(block):
        for r in rows:
            yield at, k, z, r
            at += 8


def pack(disp, spec, yup, ydown, *refs):
    blocks, own = refs[: len(BLOCKS)], refs[len(BLOCKS) :]
    for h, at in halves():
        rows = own[h]
        rows[0 : 6 * CZ * CY, :] = disp[:, at]
        rows[6 * CZ * CY : 7 * CZ * CY, :] = spec[:, at].astype(f32)
        rows[7 * CZ * CY :, :] = jnp.zeros((CZ * CY, 128), f32)
        for dst, first in ((yup, CY - W), (ydown, 0)):
            for r in range(W):
                for z in range(CZ):
                    to = (r * CZ + z) * 8
                    dst[to : to + 8, at] = rows[pl.ds(z * CY + first + r, 8, stride=CZ * CY), :]
    for dst, block in zip(blocks, BLOCKS):
        for k, (z, _) in enumerate(block):
            for ch in range(7):
                to, first = k * PLANE + ch * CY, (ch * CZ + z) * CY
                for h, at in halves():
                    dst[to : to + CY, at] = own[h][first : first + CY, :]


def y_halo(ylo, yhi, r, z, at=slice(None)):
    src = ylo if r < W else yhi
    return src[pl.ds((r % W) * CZ * 8 + z * 8, 8), at]


def pack_halo(ylo, yhi, *refs):
    for dst, block in zip(refs[len(BLOCKS) :], BLOCKS):
        for at, _, z, r in halo_at(block):
            dst[at : at + 8, :] = y_halo(ylo, yhi, r, z)


def lanes():
    return lax.broadcasted_iota(jnp.int32, (8, 128), 1)


def x_before(v):
    r = pltpu.roll(v, 1, 1)
    return jnp.where(lanes() == 0, pltpu.roll(r, 4, 0), r)


def x_after(v):
    r = pltpu.roll(v, 127, 1)
    return jnp.where(lanes() == 127, pltpu.roll(r, 4, 0), r)


def dot(a, b):
    return a[0] * b[0] + a[1] * b[1] + a[2] * b[2]


def loop(n, body, unroll=1):
    def step(k, carry):
        for q in range(unroll):
            body(k * unroll + q)
        return carry

    full = n // unroll
    if full > 1:
        lax.fori_loop(0, full, step, 0)
    else:
        full = 0
    for q in range(full * unroll, n):
        body(q)


def fill_plane(field, both, z, natural, halo):
    for h, at in halves():
        rows = both[h]
        for ch in range(7):
            rows[ch * 32 + 8 : ch * 32 + 24, :] = natural(ch, h, at)
        for r, y in enumerate(ROWS):
            if halo(r, at) is not None:
                rows[pl.ds(y + 8, 8, stride=32), :] = halo(r, at)
        for ch in range(7):
            for i in range(IE):
                first = ch * 32 + 8 - W + i
                v = rows[pl.ds(first, 4, stride=4), :]
                field[ch, z, i, 4 * h : 4 * h + 4, :] = v + H if 3 <= ch < 6 else v


def fill_block(field, both, src, block, k, z):
    places = {r: at for at, n, _, r in halo_at(block) if n == k}
    fill_plane(
        field,
        both,
        z,
        lambda ch, h, at: src[pl.ds(k * PLANE + ch * CY, CY), at],
        lambda r, at: src[pl.ds(places[r], 8), at] if r in places else None,
    )


def cation_constants(field, kc, z):
    for i in range(1, IE):
        indium = field[6, z, i] < 0.5

        def pick(fn):
            return jnp.where(indium, fn(0.848, 0.132, 4.28), fn(1.0, 0.215, 4.0)).astype(f32)

        kc[0, z, i] = pick(lambda a, b, l: 0.75 * a / l**2)
        kc[1, z, i] = pick(lambda a, b, l: -0.75 * a)
        kc[2, z, i] = pick(lambda a, b, l: 0.75 * b / l**2)
        kc[3, z, i] = pick(lambda a, b, l: 0.25 * b)
        kc[4, z, i] = pick(lambda a, b, l: l**2 / (3.0 * a))
        kc[5, z, i] = pick(lambda a, b, l: l**2 / (1.5 * b))


def anion_constants(field, ka, kl, z):
    for i in range(0, IE - 1):
        s = (field[6, z, i], x_after(field[6, z, i]), field[6, z, i + 1], field[6, z + 1, i])
        for q, (j, l) in enumerate(PAIRS):
            t = s[j] + s[l]

            def pick(fn):
                ii = fn(0.264, 4.28 * 4.28)
                mixed = fn(0.347, 4.28 * 4.0)
                gg = fn(0.43, 16.0)
                return jnp.where(t < 0.5, ii, jnp.where(t < 1.5, mixed, gg)).astype(f32)

            ka[q, z, i] = pick(lambda b, ll: 0.375 * b / ll)
            ka[6 + q, z, i] = pick(lambda b, ll: 0.125 * b)
            if W <= i < W + 4:
                kl[q, z, i - W] = pick(lambda b, ll: ll / 3.0)


OFFSETS = ((0, 0), (0, 0), (0, 1), (1, 0))


class Tiles:
    def __init__(self, ref, planes, cells):
        self.ref, self.planes, self.cells = ref, planes, cells

    def at(self, key):
        n, k, i = key
        return (n * self.planes + k) * self.cells + i

    def __getitem__(self, key):
        return self.ref[self.at(key)]

    def __setitem__(self, key, value):
        self.ref[self.at(key)] = value


def bonds(pos, z, i, which, h):
    found = {}
    cat = [pos(m, z, i) for m in range(3)]
    lo, hi = cat, (cat if h == 0 else [c + 2.0 * h for c in cat])
    for j in which:
        dz, di = OFFSETS[j]
        b = []
        for m in range(3):
            a = pos(3 + m, z - dz, i - di)
            if j == 1:
                a = x_before(a)
            b.append(a - (lo[m] if SIGNS[j][m] > 0 else hi[m]))
        found[j] = b
    return found


def cation_terms(b, k, which, energy):
    e = {}
    for j in range(4):
        for l in range(j, 4):
            if j not in which and l not in which:
                continue
            d = dot(b[j], b[l])
            e[j, l] = e[l, j] = k[0] * d + k[1] if j == l else k[2] * d + k[3]
    f = {j: [sum(e[j, l] * b[l][m] for l in range(4)) for m in range(3)] for j in which}
    total = None
    if energy:
        diag = sum(e[j, j] * e[j, j] for j in range(4))
        off = sum(e[p] * e[p] for p in PAIRS)
        total = diag * k[4] + off * k[5]
    return f, total


def anion_terms(b, k, lengths, which):
    c, total = {}, None
    for q, (j, l) in enumerate(PAIRS):
        if j not in which and l not in which:
            continue
        d = dot(b[j], b[l])
        c[j, l] = c[l, j] = k[q] * d + k[6 + q]
        if lengths is not None:
            part = c[j, l] * (d + lengths[q])
            total = part if total is None else total + part
    r = {j: [sum(c[j, l] * b[l][m] for l in range(4) if l != j) for m in range(3)] for j in which}
    return r, total


class Kind:
    def __init__(self, pos, step, emit, cells, e_row, scratch, consts, acc, low, high):
        self.pos, self.step, self.emit, self.e_row = pos, step, emit, e_row
        self.ia, self.ib = cells
        self.kc, self.ka, self.kl = consts
        self.acc, self.low, self.high = acc, low, high
        self.four = range(1 if step is None else 4)
        self.count = len(self.four)
        planes = CZ if step is None else 4
        width = self.ib - self.ia + 3
        self.bs, self.ds, self.fs, self.rs = (Tiles(ref, planes, width) for ref in scratch)
        self.counted = 0 if step is None else 1

    def here(self, z, i, which):
        b = bonds(self.pos, z, i, which, H)
        return b, None if self.step is None else bonds(self.step, z, i, which, 0)

    def keep(self, k, i, both, which):
        c = i - self.ia + 1
        for dst, v in zip((self.bs, self.ds), both):
            if v is not None:
                for j in which:
                    for m in range(3):
                        dst[3 * j + m, k, c] = x_after(v[j][m]) if j == 1 else v[j][m]

    def kept(self, k, i):
        c = i - self.ia + 1
        both = [self.bs, self.ds] if self.step is not None else [self.bs]
        return [{j: [src[3 * j + m, k + OFFSETS[j][0], c + OFFSETS[j][1]] for m in range(3)] for j in range(4)} for src in both]

    def onward(self, both):
        b, d = both[0], both[1] if len(both) > 1 else None
        return b if d is None else {j: [b[j][m] + d[j][m] for m in range(3)] for j in b}

    def cation(self, z, i, which, energy):
        both = self.here(z, i, range(4))
        consts = [self.kc[n, z, i] for n in range(6 if energy else 4)]
        found, total, b = [], None, both[0]
        for n in self.four:
            f, e = cation_terms(b, consts, which, energy and n == self.counted)
            found.append(f)
            total = e if e is not None else total
            if n + 1 < self.count:
                b = self.onward((b, both[1]))
        return both, found, total

    def anion(self, both, z, i, which, energy):
        need = [q for q, p in enumerate(PAIRS) if p[0] in which or p[1] in which]
        consts = {q + o: self.ka[q + o, z, i] for q in need for o in (0, 6)}
        lengths = [self.kl[q, z, i - W] for q in range(6)] if energy else None
        found, total, b = [], None, both[0]
        for n in self.four:
            r, e = anion_terms(b, consts, lengths if n == self.counted else None, which)
            found.append(r)
            total = e if e is not None else total
            if n + 1 < self.count:
                b = self.onward((b, both[1]))
        return found, total

    def keep_forces(self, k, i, found):
        for n, f in enumerate(found):
            for j in f:
                for m in range(3):
                    self.fs[12 * n + 3 * j + m, k, i - self.ia + 1] = f[j][m]

    def owned(self, i):
        return W <= i < W + 4

    def tally(self, totals, scale, inside=None):
        totals = [t for t in totals if t is not None]
        if totals:
            total = scale * sum(totals[1:], totals[0])
            self.acc[self.e_row] += total if inside is None else jnp.where(inside, total, 0.0)

    def cation_plane(self, z, k, inside, bonds_at_start, kept):
        own = inside is not False
        totals = []
        if bonds_at_start:
            self.keep(k, self.ia - 1, self.here(z, self.ia - 1, bonds_at_start), bonds_at_start)
        for i in range(self.ia, self.ib + 1):
            both, f, e = self.cation(z, i, range(4), own and self.owned(i))
            self.keep(k, i, both, kept)
            self.keep_forces(k, i, f)
            totals.append(e)
        both, f, _ = self.cation(z, self.ib + 1, (2,), False)
        if 2 in kept:
            self.keep(k, self.ib + 1, both, (2,))
        self.keep_forces(k, self.ib + 1, f)
        self.tally(totals, 1.0, None if inside is True else inside)

    def bond_plane(self, z, k):
        for i in range(self.ia - 1, self.ib + 2):
            which = ((0, 1) if i <= self.ib else ()) + ((2,) if i >= self.ia else ())
            self.keep(k, i, self.here(z, i, which), which)

    def anion_plane(self, z, k, inside, take):
        own = inside is not False
        totals = []
        r, _ = self.anion(self.kept(k, self.ia - 1), z, self.ia - 1, (2,), False)
        before = [q[2] for q in r]
        for i in range(self.ia, self.ib + 1):
            r, e = self.anion(self.kept(k, i), z, i, range(4), own and self.owned(i))
            for n in self.four:
                for m in range(3):
                    q = [r[n][j][m] for j in range(4)]
                    take(n, m, i, q[0] + x_before(q[1]) + before[n][m], (q[0] + q[1]) + (q[2] + q[3]), q[3])
            before = [q[2] for q in r]
            totals.append(e)
        self.tally(totals, 0.5, None if inside is True else inside)

    def forces(self, k, i, n, m):
        c = i - self.ia + 1
        f = [self.fs[12 * n + 3 * j + m, k, c] for j in range(4)]
        return (f[0] + f[1]) + (f[2] + f[3]), f[0] + x_after(f[1]) + self.fs[12 * n + 6 + m, k, c + 1], f[3]

    def inner(self, za, zb, unroll):
        rs, ia, ib = self.rs, self.ia, self.ib
        count = zb - za + 1
        every = (0, 1, 2, 3)

        def cations(q):
            self.cation_plane(za + q, 1 + q, True, (0, 1, 3), every)

        loop(count, cations, unroll)
        self.cation_plane(zb + 1, count + 1, True, (0, 1, 3), every)
        self.bond_plane(za - 1, 0)

        def below(n, m, i, to_cation, to_anion, last):
            c = i - ia
            rs[3 * n + m, 0, c + 1] = last
            self.low[n, m, c] = to_cation
            self.low[n, 3 + m, c] = to_anion

        self.anion_plane(za - 1, 0, True, below)

        def anions(q):
            z, k = za + q, 1 + q

            def take(n, m, i, to_cation, to_anion, last):
                own, ahead, _ = self.forces(k, i, n, m)
                c = i - ia + 1
                rs[3 * n + m, k, c] = last
                self.emit(n, m, z, i, own + to_cation + rs[3 * n + m, k - 1, c])
                self.emit(n, 3 + m, z, i, ahead + self.fs[12 * n + 9 + m, k + 1, c] + to_anion)

            self.anion_plane(z, k, True, take)

        for q in range(count):
            anions(q)
        for i in range(ia, ib + 1):
            c = i - ia
            for n in self.four:
                for m in range(3):
                    self.low[n, 6 + m, c] = self.fs[12 * n + 9 + m, 1, c + 1]
                    own, ahead, _ = self.forces(count + 1, i, n, m)
                    self.high[n, m, c] = own
                    self.high[n, 3 + m, c] = ahead
                    self.high[n, 6 + m, c] = rs[3 * n + m, count, c + 1]
        self.keep_high(count + 1)

    def keep_high(self, k):
        for c in range(self.ib - self.ia + 3):
            for j in range(9):
                self.high[self.count, j, c] = self.bs[j, k, c]
                if self.step is not None:
                    self.high[self.count + 1, j, c] = self.ds[j, k, c]

    def lower(self, z):
        rs, ia, ib = self.rs, self.ia, self.ib
        self.cation_plane(z, 1, own_plane(z), (3,), (3,))
        self.bond_plane(z - 1, 0)

        def take(n, m, i, to_cation, to_anion, last):
            c = i - ia
            own, ahead, third = self.forces(1, i, n, m)
            self.emit(n, m, z, i, own + self.low[n, m, c] + last)
            self.emit(n, 3 + m, z, i, ahead + self.low[n, 6 + m, c] + self.low[n, 3 + m, c])
            self.low[n, m, c] = to_cation
            self.low[n, 3 + m, c] = to_anion
            self.low[n, 6 + m, c] = third

        self.anion_plane(z - 1, 0, own_plane(z - 1), take)

    def upper(self, z):
        ia, ib = self.ia, self.ib
        for c in range(ib - ia + 3):
            for j in range(9):
                self.bs[j, 2, c] = self.high[self.count, j, c]
                if self.step is not None:
                    self.ds[j, 2, c] = self.high[self.count + 1, j, c]
        self.cation_plane(z + 1, 3, own_plane(z + 1), (0, 1, 3), (0, 1, 2, 3))

        def take(n, m, i, to_cation, to_anion, last):
            c = i - ia
            own, ahead, third = self.forces(3, i, n, m)
            self.emit(n, m, z, i, self.high[n, m, c] + to_cation + self.high[n, 6 + m, c])
            self.emit(n, 3 + m, z, i, self.high[n, 3 + m, c] + third + to_anion)
            self.high[n, m, c] = own
            self.high[n, 3 + m, c] = ahead
            self.high[n, 6 + m, c] = last

        self.anion_plane(z, 2, own_plane(z), take)
        self.keep_high(3)


def own_plane(z):
    return W <= z < W + CZ


def kinds(steps, state, scratch):
    field, g0, pos1, g1, pos2, step, gs, kc, ka, kl, acc, *ends = state
    bs, fs, rs, ds = scratch[:4]
    s0, s1 = steps[0], steps[1]
    consts = (kc, ka, kl)

    def emit0(n, m, z, i, v):
        g0[m, z, i] = v
        pos1[m, z, i] = field[m, z, i] + s0 * v if m < 3 else field[m, z, i] - s0 * v

    def emit1(n, m, z, i, v):
        g1[m, z - 2, i - 2] = v
        w, d = s1 * g0[m, z, i], s1 * v
        pos2[m, z - 2, i - 2] = (pos1[m, z, i] + d) - w if m < 3 else (pos1[m, z, i] - d) + w
        step[m, z - 2, i - 2] = w if m < 3 else -w

    def emit2(n, m, z, i, v):
        gs[n, m, z - W, i - W] = v

    def at(ref):
        return lambda m, z, i: ref[m, z - 2, i - 2]

    work = (bs, ds, fs, rs)
    return (
        Kind(lambda m, z, i: field[m, z, i], None, emit0, (1, IE - 2), E0, work, consts, acc, *ends[0:2]),
        Kind(lambda m, z, i: pos1[m, z, i], None, emit1, (2, IE - 3), E1, work, consts, acc, *ends[2:4]),
        Kind(at(pos2), at(step), emit2, (W, IE - W - 1), ES + 1, work, consts, acc, *ends[4:6]),
    )


def products(state, planes):
    g0, g1, gs, acc = state[1], state[3], state[6], state[10]
    part = [None] * SUMS

    def add(n, v):
        part[n] = v if part[n] is None else part[n] + v

    for z in planes:
        for i in range(W, W + 4):
            for ch in range(6):
                a, b = g0[ch, z, i], g1[ch, z - 2, i - 2]
                g = [gs[k, ch, z - W, i - W] for k in range(4)]
                add(N0, a * a)
                add(N1, b * b)
                add(X1, a * b)
                for k in range(4):
                    add(GG1 + k, g[k] * b)
                    add(GG0 + k, g[k] * a)
                for n, (k, l) in enumerate(GPAIRS):
                    add(GG + n, g[k] * g[l])
    for n, v in enumerate(part):
        if v is not None:
            acc[n] += v


def stage_inner(own0, own1, ylo, yhi, steps, *refs):
    state, scratch = refs[:STATE], refs[STATE:]
    field, kc, ka, kl, acc = state[0], *state[7:11]
    own = (own0, own1)
    acc[...] = jnp.zeros_like(acc)

    def fill(z):
        def natural(ch, h, at):
            return own[h][pl.ds((ch * CZ + z) * CY, CY), :]

        fill_plane(field, scratch[4:6], W + z, natural, lambda r, at: y_halo(ylo, yhi, r, z, at))

    loop(CZ, fill)
    loop(CZ, lambda z: cation_constants(field, kc, W + z))
    loop(CZ - 1, lambda z: anion_constants(field, ka, kl, W + z))
    top = W + CZ - 1
    first, second, third = kinds(steps, state, scratch)
    first.inner(W + 1, top - 1, 2)
    second.inner(W + 2, top - 2, 2)
    third.inner(W + 3, top - 3, 1)
    products(state, (W + 3, top - 3))


def stage_outer(levels, below, above, steps, *refs):
    state, rest = refs[STATE : 2 * STATE], refs[2 * STATE :]
    final = levels[-1] == W
    scratch = rest[1:] if final else rest
    field, kc, ka, kl, acc = state[0], *state[7:11]
    for k, level in enumerate(levels):
        lo, hi = W - level, W + CZ - 1 + level
        fill_block(field, scratch[4:6], below, UP[levels[0] - 1 : levels[-1]], k, lo)
        fill_block(field, scratch[4:6], above, DOWN[levels[0] - 1 : levels[-1]], k, hi)
        if level < W:
            cation_constants(field, kc, lo)
        cation_constants(field, kc, hi)
        for z in (lo, hi - 1):
            anion_constants(field, ka, kl, z)
        for n, kind in enumerate(kinds(steps, state, scratch)):
            kind.lower(lo + 1 + n)
            kind.upper(hi - 1 - n)
        products(state, (lo + W, hi - W))
    if not final:
        return
    sums = rest[0]
    partial = jnp.sum(acc[...], axis=1)
    row = lax.broadcasted_iota(jnp.int32, (SUMS, 128), 0)
    lane = lax.broadcasted_iota(jnp.int32, (SUMS, 128), 1)
    spread = jnp.where(row == lane, jnp.sum(partial, axis=1, keepdims=True), 0.0)
    sums[...] = jnp.broadcast_to(jnp.sum(spread, axis=0, keepdims=True), sums.shape)


def finish(cell_count, gathered, steps, g0, pos1, g1, gs, out_hbm, energies, rows0, rows1, out, sems):
    total = jnp.sum(gathered[...], axis=0, keepdims=True)

    def pick(n):
        return total[:, n : n + 1]

    t = (pick(N1) - pick(X1)) / (pick(N0) + 1e-06)
    lag = (
        -t * (t - 1.0) * (t - 2.0) * (1.0 / 6.0),
        (t + 1.0) * (t - 1.0) * (t - 2.0) * 0.5,
        -(t + 1.0) * t * (t - 2.0) * 0.5,
        (t + 1.0) * t * (t - 1.0) * (1.0 / 6.0),
    )
    t2, t3, t4 = t * t, t * t * t, t * t * t * t
    area = (
        -(t4 * 0.25 - t3 + t2) * (1.0 / 6.0),
        (t4 * 0.25 - t3 * (2.0 / 3.0) - t2 * 0.5 + 2.0 * t) * 0.5,
        -(t4 * 0.25 - t3 * (1.0 / 3.0) - t2) * 0.5,
        (t4 * 0.25 - t2 * 0.5) * (1.0 / 6.0),
    )
    norm2 = sum((1.0 if k == l else 2.0) * lag[k] * lag[l] * pick(GG + n) for n, (k, l) in enumerate(GPAIRS))
    cross2 = sum(lag[k] * pick(GG1 + k) for k in range(4))
    ratio = (norm2 - cross2) / (pick(N1) + 1e-06)
    s1, s2 = steps[1][0:1, 0:1], steps[2][0:1, 0:1]
    energy2 = pick(ES + 1) - s1 * sum(area[k] * pick(GG0 + k) for k in range(4))
    scale = 1.0 / cell_count
    energies[0] = jnp.sum(pick(E0)) * scale
    energies[1] = jnp.sum(pick(E1)) * scale
    energies[2] = jnp.sum(energy2) * scale
    along = s1 + s2 * ratio
    weights = [jnp.broadcast_to(w, (8, 128)) for w in [s2 * q for q in lag] + [along * t, along]]

    copies = []
    for ch in range(6):

        def plane(z):
            for i in range(4):
                parts = [gs[k, ch, z, i] for k in range(4)]
                parts += [g0[ch, z + W, i + W], g1[ch, z + 1, i + 1]]
                v = pos1[ch, z + W, i + W]
                for weight, part in zip(weights, parts):
                    v = v + weight * part if ch < 3 else v - weight * part
                if ch >= 3:
                    v = v - H
                rows0[pl.ds(z * CY + i, 4, stride=4), :] = v[0:4]
                rows1[pl.ds(z * CY + i, 4, stride=4), :] = v[4:8]

        loop(CZ, plane, 2)
        to = slice(ch * CZ * CY, (ch + 1) * CZ * CY)
        for h, at in halves():
            out[to, at] = (rows0, rows1)[h][...]
        copies.append(pltpu.make_async_copy(out.at[to], out_hbm.at[to], sems.at[ch]))
        copies[-1].start()
    for copy in copies:
        copy.wait()


def vmem():
    return pl.BlockSpec(memory_space=pltpu.VMEM)


def smem():
    return pl.BlockSpec(memory_space=pltpu.SMEM)


def params(mib):
    return pltpu.CompilerParams(vmem_limit_bytes=mib * MIB)


def ring(value, axis, step):
    n = lax.axis_size(axis)
    return lax.ppermute(value, axis, [(i, (i + step) % n) for i in range(n)])


def per_device(displacement, species, step_sizes):
    shape = jax.ShapeDtypeStruct
    devices = lax.axis_size("slab") * lax.axis_size("col")
    cell_count = devices * CZ * CY * NX
    disp = displacement.reshape(6 * CZ * CY, NX)
    spec = species.reshape(CZ * CY, NX)
    edge = shape((W * CZ * 8, NX), f32)
    blocks = tuple(shape((block_rows(block), NX), f32) for block in BLOCKS)
    half = shape((8 * CZ * CY, 128), f32)
    yup, ydown, *packed = pl.pallas_call(
        pack,
        out_shape=(edge, edge, *blocks, half, half),
        in_specs=[vmem()] * 2,
        out_specs=[vmem()] * (4 + len(blocks)),
        compiler_params=params(4),
        name="pack",
    )(disp, spec)
    own = packed[-2:]
    _, step_sizes = lax.optimization_barrier((own[0], step_sizes))
    steps = jnp.broadcast_to(step_sizes[:, None, None], (3, 8, 128))
    ylo, yhi = ring(yup, "col", 1), ring(ydown, "col", -1)
    ups = pl.pallas_call(
        pack_halo,
        out_shape=blocks,
        in_specs=[vmem()] * (2 + len(blocks)),
        out_specs=[vmem()] * len(blocks),
        input_output_aliases={2 + n: n for n in range(len(blocks))},
        compiler_params=params(4),
        name="pack_halo",
    )(ylo, yhi, *packed[: len(blocks)])

    def travel(level):
        return ring(ups[2 * level], "slab", 1), ring(ups[2 * level + 1], "slab", -1)

    def tiles(*lead):
        return (*lead, 8, 128)

    state_shapes = tuple(
        shape(tiles(*lead), f32)
        for lead in (
            (7, ZE, IE),
            (6, ZE, IE),
            (6, ZE, IE),
            (6, ZE - 4, IE - 4),
            (6, ZE - 4, IE - 4),
            (6, ZE - 4, IE - 4),
            (4, 6, CZ, 4),
            (6, ZE, IE),
            (12, ZE - 1, IE - 1),
            (6, ZE, 4),
            (SUMS,),
            (1, 9, 8),
            (2, 9, 10),
            (1, 9, 6),
            (2, 9, 8),
            (4, 9, 4),
            (6, 9, 6),
        )
    )
    scratch = [
        pltpu.VMEM(tiles(12 * CZ * IE), f32),
        pltpu.VMEM(tiles(48 * 4 * 6), f32),
        pltpu.VMEM(tiles(3 * CZ * IE + 48), f32),
        pltpu.VMEM(tiles(12 * 4 * 6), f32),
        pltpu.VMEM((8 * 32, 128), f32),
        pltpu.VMEM((8 * 32, 128), f32),
    ]
    near = travel(0)
    state = pl.pallas_call(
        stage_inner,
        out_shape=state_shapes,
        in_specs=[vmem()] * 5,
        out_specs=[vmem()] * STATE,
        scratch_shapes=scratch,
        compiler_params=params(17),
        cost_estimate=pl.CostEstimate(flops=100000000, bytes_accessed=1000000, transcendentals=0),
        name="stage_inner",
    )(*own, ylo, yhi, steps)
    state = list(state)
    *last, state[10] = lax.optimization_barrier((*ups[2:4], state[10]))
    ups = (*ups[:2], *last)
    for levels, arrived in (((1, 2), near), ((3,), travel(1))):
        final = levels[-1] == W
        state = pl.pallas_call(
            functools.partial(stage_outer, levels),
            out_shape=(*state_shapes, shape((devices, 128), f32)) if final else state_shapes,
            in_specs=[vmem()] * (3 + STATE),
            out_specs=[vmem()] * (STATE + final),
            scratch_shapes=scratch,
            input_output_aliases={3 + n: n for n in range(STATE)},
            compiler_params=params(17),
            cost_estimate=pl.CostEstimate(flops=100000000, bytes_accessed=1000000, transcendentals=0),
            name="stage_outer",
        )(*arrived, steps, *state)
    *state, sums = state
    gathered = lax.all_to_all(sums.reshape(devices, 1, 128), ("slab", "col"), 0, 0)
    relaxed, energies = pl.pallas_call(
        functools.partial(finish, cell_count),
        out_shape=(shape((6 * CZ * CY, NX), f32), shape((3,), f32)),
        in_specs=[vmem()] * 6,
        out_specs=[pl.BlockSpec(memory_space=pltpu.HBM), smem()],
        scratch_shapes=[
            pltpu.VMEM((CZ * CY, 128), f32),
            pltpu.VMEM((CZ * CY, 128), f32),
            pltpu.VMEM((6 * CZ * CY, NX), f32),
            pltpu.SemaphoreType.DMA((6,)),
        ],
        compiler_params=params(4),
        name="finish",
    )(gathered.reshape(devices, 128), steps, *state[1:4], state[6])
    return relaxed.reshape(displacement.shape), energies


def solution(mesh):
    in_specs = (P(None, "slab", "col", None), P("slab", "col", None), P())
    out_specs = (P(None, "slab", "col", None), P())
    return jax.shard_map(
        per_device, mesh=mesh, in_specs=in_specs, out_specs=out_specs, check_vma=False
    )
```
